32 devices in a mesh: gz: 8 (over z, y), gy: 4 (over x, core).
Axes of the slice: x: 2, y: 2, z: 4, core: 2. Of those that a mesh axis runs over, the one named last changes fastest.
Arguments:
- species_field: float32 [4, 512, 512, 512], P(None, 'gz', 'gy'), may hold values from -100 to 100
Outputs:
- core_tensor: float32 [4, 512, 4096], P(None, ('gz', 'gy'))
- basis_z: float32 [512, 64], replicated
- basis_y: float32 [512, 64], replicated
The draws below stay inside these ranges and needn't reach their ends.
All inputs are finite; a program needn't handle non-finite values.
Results may differ from the reference program's by a relative error of at most 0.0003.
Values sent between devices are 32-bit elements; how exact they have to be, the bound alone decides.
No kernel may reach another device: no remote copies, remote signals or barrier semaphores. Data moves between devices by JAX's collectives and lax.ppermute only.
A program may use at most 320 MiB of HBM per device.

```python
import math
import jax
import jax.numpy as jnp
from jax import lax

SPECIES = 4
GRID = 512
RANK = 64
ITERS = 4
NX = 512


def draw_species_field(key, part):
    key_noise, key_u, key_v, key_w, key_y, key_z = jax.random.split(key, 6)
    mode_count = 2 * RANK
    shape_all = (SPECIES, GRID, GRID, NX)
    mode_index = jnp.arange(mode_count).astype(jnp.float32)
    top_level = 8.0
    fall_off = math.log(0.1)
    noise_values = jnp.clip(jax.random.normal(key_noise, shape_all, jnp.float32), -6.0, 6.0)
    along_z = jnp.clip(jax.random.normal(key_u, (mode_count, GRID), jnp.float32), -6.0, 6.0)
    along_y = jnp.clip(jax.random.normal(key_v, (mode_count, GRID), jnp.float32), -6.0, 6.0)
    along_x = jnp.clip(jax.random.normal(key_w, (mode_count, SPECIES, NX), jnp.float32), -6.0, 6.0)
    scale_y = jnp.exp(jax.random.uniform(key_y, (GRID,), jnp.float32, 0.0, math.log(1.4)))
    scale_z = jnp.exp(jax.random.uniform(key_z, (GRID,), jnp.float32, 0.0, math.log(1.4)))
    amplitude = jnp.sqrt(top_level * jnp.exp(fall_off * mode_index / mode_count) / GRID)
    plane_modes = along_z[:, :, None] * along_y[:, None, :] * amplitude[:, None, None]
    signal_part = jnp.einsum('kzy,ksx->szyx', plane_modes, along_x, precision=lax.Precision.HIGHEST)
    field_values = (signal_part + noise_values) * scale_z[None, :, None, None] * scale_y[None, None, :, None]
    return jnp.clip(field_values, -100.0, 100.0)


def setup_inputs(seed: int = 0) -> dict:
    key_list = jax.random.split(jax.random.key(seed), 2)
    species_field = draw_species_field(jax.random.fold_in(key_list[1], 71), 0)
    return {"species_field": species_field}


def start_table(order, width):
    row_index = jnp.arange(order).astype(jnp.float32)
    col_index = jnp.arange(width).astype(jnp.float32)
    return jnp.cos(math.pi * (row_index[:, None] + 0.5) * col_index[None, :] / order)

def refine_basis(matrix, current):
    product = jnp.dot(matrix, current, precision=lax.Precision.HIGHEST)
    inner_gram = lax.dot_general(product, product, (((0,), (0,)), ((), ())), precision=lax.Precision.HIGHEST)
    factor = jnp.linalg.cholesky(inner_gram)
    return lax.linalg.triangular_solve(factor, product, left_side=False, lower=True, transpose_a=True)

def leaf_basis(gram_matrix):
    basis_now = start_table(GRID, RANK)
    for iteration in range(ITERS):
        basis_now = refine_basis(gram_matrix, basis_now)
    return basis_now

def mode_gram(fibres, mode):
    others = tuple((d for d in range(4) if d != mode))
    return lax.dot_general(fibres, fibres, ((others, others), ((), ())), precision=lax.Precision.HIGHEST)

def reference(species_field):
    gram_z = mode_gram(species_field, 1)
    basis_z = leaf_basis(gram_z)
    reduced = jnp.einsum('szyx,zr->sryx', species_field, basis_z, precision=lax.Precision.HIGHEST)
    gram_y = mode_gram(reduced, 2)
    basis_y = leaf_basis(gram_y)
    core_tensor = jnp.einsum('sryx,yq->sxrq', reduced, basis_y, precision=lax.Precision.HIGHEST)
    core_tensor = core_tensor.reshape(SPECIES, NX, RANK * RANK)
    return (core_tensor, basis_z, basis_y)
```

```python
import functools
import math

import jax
import jax.numpy as jnp
from jax import lax
from jax.experimental import pallas as pl
from jax.experimental.pallas import tpu as pltpu
from jax.sharding import PartitionSpec as P

RANK = 64
ITERS = 4
CORES = 2
AXES = ("gz", "gy")
DEPTH = 6
MIB = 1 << 20
F32 = jnp.float32
BF16 = jnp.bfloat16


def start_table(order, width):
    row_index = jnp.arange(order).astype(jnp.float32)
    col_index = jnp.arange(width).astype(jnp.float32)
    return jnp.cos(math.pi * (row_index[:, None] + 0.5) * col_index[None, :] / order)


def tie(value, other):
    return lax.optimization_barrier((value, other))[0]


def split_bf16(value):
    high = value.astype(BF16)
    low = (value - high.astype(F32)).astype(BF16)
    return high, low


def dot_nn(left, right):
    return lax.dot_general(left, right, (((1,), (0,)), ((), ())), preferred_element_type=F32)


def dot_nt(left, right):
    return lax.dot_general(left, right, (((1,), (1,)), ((), ())), preferred_element_type=F32)


def dot_tn(left, right):
    return lax.dot_general(left, right, (((0,), (0,)), ((), ())), preferred_element_type=F32)


def pack_kernel(groups, width, me_ref, field_ref, *out_refs):
    turned = out_refs[-1]
    me = me_ref[0]
    for z in range(field_ref.shape[1]):
        turned[...] = field_ref[0, z].T
        for k in range(groups):
            start = pl.multiple_of((me ^ k) * width, width)
            out_refs[k][:, z, :] = turned[pl.ds(start, width), :]


def pack(field, me, species, groups):
    _, z_n, y_n, x_n = field.shape
    width = x_n // groups
    z_tile = 8
    return pl.pallas_call(
        functools.partial(pack_kernel, groups, width),
        grid_spec=pltpu.PrefetchScalarGridSpec(
            num_scalar_prefetch=1,
            grid=(z_n // z_tile,),
            in_specs=[pl.BlockSpec((1, z_tile, y_n, x_n), lambda i, m: (species, i, 0, 0))],
            out_specs=[pl.BlockSpec((width, z_tile, y_n), lambda i, m: (0, i, 0))] * groups,
            scratch_shapes=[pltpu.VMEM((x_n, y_n), F32)],
        ),
        out_shape=[jax.ShapeDtypeStruct((width, z_n, y_n), F32)] * groups,
        compiler_params=pltpu.CompilerParams(vmem_limit_bytes=24 * MIB),
        cost_estimate=pl.CostEstimate(
            flops=0, bytes_accessed=4 * 8 * z_n * y_n * x_n, transcendentals=0),
        name="pack",
    )(me, field)


def gram_z_kernel(groups, side, me_ref, prev_ref, *refs):
    pieces, out_ref, (high, low, sum_hh, sum_hl) = refs[:groups], refs[groups], refs[groups + 1:]
    step = pl.program_id(0)
    me_z = me_ref[0] // side
    x_tile, z_n, y_n = pieces[0].shape

    @pl.when(step == 0)
    def _():
        sum_hh[...] = jnp.zeros_like(sum_hh)
        sum_hl[...] = jnp.zeros_like(sum_hl)

    for k in range(groups):
        row = pl.multiple_of((me_z ^ (k // side)) * z_n, z_n)
        for x in range(x_tile):
            col = (x * side + k % side) * y_n
            high_part, low_part = split_bf16(pieces[k][x])
            high[pl.ds(row, z_n), col:col + y_n] = high_part
            low[pl.ds(row, z_n), col:col + y_n] = low_part
    sum_hh[...] += dot_nt(high[...], high[...])
    sum_hl[...] += dot_nt(high[...], low[...])

    @pl.when(step == pl.num_programs(0) - 1)
    def _():
        cross = sum_hl[...]
        out_ref[...] = prev_ref[...] + (sum_hh[...] + (cross + cross.T))


def gram_z_step(prev, pieces, me, side):
    groups = len(pieces)
    width, z_n, y_n = pieces[0].shape
    order = z_n * (groups // side)
    x_tile = 4
    depth = x_tile * side * y_n
    whole = pl.BlockSpec((order, order), lambda i, m: (0, 0))
    return pl.pallas_call(
        functools.partial(gram_z_kernel, groups, side),
        grid_spec=pltpu.PrefetchScalarGridSpec(
            num_scalar_prefetch=1,
            grid=(width // x_tile,),
            in_specs=[whole] + [pl.BlockSpec((x_tile, z_n, y_n), lambda i, m: (i, 0, 0))] * groups,
            out_specs=whole,
            scratch_shapes=[pltpu.VMEM((order, depth), BF16), pltpu.VMEM((order, depth), BF16),
                            pltpu.VMEM((order, order), F32), pltpu.VMEM((order, order), F32)],
        ),
        out_shape=jax.ShapeDtypeStruct((order, order), F32),
        compiler_params=pltpu.CompilerParams(vmem_limit_bytes=32 * MIB),
        cost_estimate=pl.CostEstimate(
            flops=4 * order * order * width * side * y_n,
            bytes_accessed=4 * groups * width * z_n * y_n, transcendentals=0),
        name="gram_z",
    )(me, prev, *pieces)


def basis_kernel(gz_n, me_ref, gram_ref, start_ref, basis_ref, turned_ref):
    rank, order = start_ref.shape
    highest = dict(precision=lax.Precision.HIGHEST, preferred_element_type=F32)
    row_id = lax.broadcasted_iota(jnp.int32, (rank, 1), 0)
    lane_id = lax.broadcasted_iota(jnp.int32, (rank, rank), 1)
    row_ids = lax.broadcasted_iota(jnp.int32, (rank, rank), 0)
    eye = jnp.where(lane_id == row_ids, 1.0, 0.0).astype(F32)

    def iterate(_, basis_t):
        product = lax.dot_general(basis_t, gram_ref[...], (((1,), (0,)), ((), ())), **highest)
        inner = lax.dot_general(product, product, (((1,), (1,)), ((), ())), **highest)
        work = jnp.concatenate([inner, eye], axis=1)
        for k in range(rank - 1):
            row = work[k:k + 1, :]
            scaled = row / work[k:k + 1, k:k + 1]
            factor = jnp.where(row_id > k, work[:, k:k + 1], 0.0)
            work = work - factor * scaled
        pivots = jnp.sum(jnp.where(lane_id == row_ids, work[:, :rank], 0.0), axis=1, keepdims=True)
        inverse = work[:, rank:] * (1.0 / jnp.sqrt(pivots))
        return lax.dot_general(inverse, product, (((1,), (0,)), ((), ())), **highest)

    basis_t = lax.fori_loop(0, ITERS, iterate, start_ref[...])
    basis_ref[...] = basis_t
    if gz_n > 1:
        me_z = me_ref[0]
        size = order // gz_n
        while size < order:
            parts = [basis_t[:, i:i + size] for i in range(0, order, size)]
            swapped = jnp.concatenate([parts[i ^ 1] for i in range(len(parts))], axis=1)
            bit = (me_z // (size // (order // gz_n))) % 2
            basis_t = jnp.where(bit == 1, swapped, basis_t)
            size *= 2
    turned_ref[...] = basis_t


def leaf_basis(gram, start_t, me_z, gz_n):
    rank, order = start_t.shape
    vmem = pl.BlockSpec(memory_space=pltpu.VMEM)
    return pl.pallas_call(
        functools.partial(basis_kernel, gz_n),
        in_specs=[pl.BlockSpec(memory_space=pltpu.SMEM), vmem, vmem],
        out_specs=[vmem, vmem],
        out_shape=[jax.ShapeDtypeStruct((rank, order), F32)] * 2,
        compiler_params=pltpu.CompilerParams(vmem_limit_bytes=24 * MIB),
        name="leaf_basis",
    )(me_z, gram, start_t)


def reduce_kernel(groups, side, pos_ref, basis_ref, *refs):
    pieces, out_ref = refs[:groups], refs[groups]
    rank = basis_ref.shape[0]
    me_x = pos_ref[1]
    x_tile, z_n, y_n = pieces[0].shape
    high, low = split_bf16(basis_ref[...])
    both = jnp.concatenate([high, low], axis=0)
    for x in range(x_tile):
        cols = [jnp.concatenate([pieces[k][x] for k in range(j, groups, side)], axis=0)
                for j in range(side)]
        field_high, field_low = split_bf16(jnp.concatenate(cols, axis=1))
        first = dot_nn(both, field_high)
        total = first[:rank] + (first[rank:] + dot_nn(high, field_low))
        for j in range(side):
            start = pl.multiple_of((me_x ^ j) * y_n, y_n)
            out_ref[x, :, pl.ds(start, y_n)] = total[:, j * y_n:(j + 1) * y_n]


def reduce_half(basis_t, pieces, pos, side):
    groups = len(pieces)
    width, z_n, y_n = pieces[0].shape
    half = width // CORES
    x_tile = 4
    rank, order = basis_t.shape
    tiles = half // x_tile
    return pl.pallas_call(
        functools.partial(reduce_kernel, groups, side),
        grid_spec=pltpu.PrefetchScalarGridSpec(
            num_scalar_prefetch=1,
            grid=(tiles,),
            in_specs=[pl.BlockSpec((rank, order), lambda i, p: (0, 0))]
            + [pl.BlockSpec((x_tile, z_n, y_n), lambda i, p: (p[0] * tiles + i, 0, 0))] * groups,
            out_specs=pl.BlockSpec((x_tile, rank, side * y_n), lambda i, p: (i, 0, 0)),
        ),
        out_shape=jax.ShapeDtypeStruct((half, rank, side * y_n), F32),
        compiler_params=pltpu.CompilerParams(vmem_limit_bytes=24 * MIB),
        cost_estimate=pl.CostEstimate(
            flops=6 * rank * order * half * side * y_n,
            bytes_accessed=4 * groups * half * z_n * y_n, transcendentals=0),
        name="reduce_z",
    )(pos, basis_t, *pieces)


def gram_y_kernel(species, side, core_ref, *refs):
    mine, others = refs[:species], refs[species:2 * species]
    full_ref, gram_ref, sum_hh, sum_hl = refs[2 * species:]
    step = pl.program_id(0)
    core = core_ref[0]
    x_tile, rank, two = mine[0].shape
    y_n = two // side

    @pl.when(step == 0)
    def _():
        sum_hh[...] = jnp.zeros_like(sum_hh)
        sum_hl[...] = jnp.zeros_like(sum_hl)

    for s in range(species):
        for j in range(side):
            for ref, place in ((mine[s], core), (others[s], 1 - core)):
                start = pl.multiple_of((j * CORES + place) * y_n, y_n)
                full_ref[s, :, :, pl.ds(start, y_n)] = ref[:, :, j * y_n:(j + 1) * y_n]
    order = full_ref.shape[-1]
    high, low = split_bf16(full_ref[...].reshape(species * x_tile * rank, order))
    sum_hh[...] += dot_tn(high, high)
    sum_hl[...] += dot_tn(high, low)

    @pl.when(step == pl.num_programs(0) - 1)
    def _():
        cross = sum_hl[...]
        gram_ref[...] = sum_hh[...] + (cross + cross.T)


def gram_y_full(mine, others, core, side):
    species = len(mine)
    half, rank, two = mine[0].shape
    order = two * CORES
    x_tile = 4
    part = pl.BlockSpec((x_tile, rank, two), lambda i, c: (i, 0, 0))
    return pl.pallas_call(
        functools.partial(gram_y_kernel, species, side),
        grid_spec=pltpu.PrefetchScalarGridSpec(
            num_scalar_prefetch=1,
            grid=(half // x_tile,),
            in_specs=[part] * (2 * species),
            out_specs=[pl.BlockSpec((species, x_tile, rank, order), lambda i, c: (0, i, 0, 0)),
                       pl.BlockSpec((order, order), lambda i, c: (0, 0))],
            scratch_shapes=[pltpu.VMEM((order, order), F32), pltpu.VMEM((order, order), F32)],
        ),
        out_shape=[jax.ShapeDtypeStruct((species, half, rank, order), F32),
                   jax.ShapeDtypeStruct((order, order), F32)],
        compiler_params=pltpu.CompilerParams(vmem_limit_bytes=40 * MIB),
        name="gram_y",
    )(core, *mine, *others)


def core_kernel(basis_ref, full_ref, out_ref):
    species, x_tile, rank, order = full_ref.shape
    high, low = split_bf16(basis_ref[...])
    field_high, field_low = split_bf16(full_ref[...].reshape(species * x_tile * rank, order))
    first = dot_nt(field_high, jnp.concatenate([high, low], axis=0))
    second = dot_nt(field_low, high)
    total = first[:, :rank] + (first[:, rank:] + second)
    out_ref[...] = total.reshape(species, x_tile, rank, rank)


def project_core(basis_t, full):
    species, half, rank, order = full.shape
    x_tile = 4
    return pl.pallas_call(
        core_kernel,
        grid=(half // x_tile,),
        in_specs=[pl.BlockSpec((rank, order), lambda i: (0, 0)),
                  pl.BlockSpec((species, x_tile, rank, order), lambda i: (0, i, 0, 0))],
        out_specs=pl.BlockSpec((species, x_tile, rank, rank), lambda i: (0, i, 0, 0)),
        out_shape=jax.ShapeDtypeStruct((species, half, rank, rank), F32),
        compiler_params=pltpu.CompilerParams(vmem_limit_bytes=24 * MIB),
        name="core",
    )(basis_t, full)


def permute(value, mask, total):
    return lax.ppermute(value, AXES, [(i, i ^ mask) for i in range(total)])


def all_sum(value, me, total, quads):
    low = total // quads
    bits = [1 << b for b in range(low.bit_length() - 1)]
    current = value
    for bit in bits:
        half = current.shape[0] // 2
        upper = (me // bit) % 2 == 1
        first, second = current[:half], current[half:]
        current = jnp.where(upper, second, first) + permute(
            jnp.where(upper, first, second), bit, total)
    place = me // low
    parts = current.reshape(quads, -1, current.shape[1])
    pick = lambda k: lax.dynamic_index_in_dim(parts, place ^ k, 0, False)
    arrived = [permute(pick(k), low * k, total) for k in range(1, quads)]
    sums = pick(0)
    for part in arrived:
        sums = sums + part
    stack = jnp.stack([sums] + [permute(sums, low * k, total) for k in range(1, quads)])
    current = jnp.concatenate(
        [lax.dynamic_index_in_dim(stack, place ^ j, 0, False) for j in range(quads)])
    for bit in reversed(bits):
        other = permute(current, bit, total)
        upper = (me // bit) % 2 == 1
        current = jnp.concatenate(
            [jnp.where(upper, other, current), jnp.where(upper, current, other)])
    return current


def send_order(gz_n, side):
    groups = gz_n * side
    far = [k for k in range(groups // 2, groups)]
    near = [k for k in range(1, groups // 2)]
    far.sort(key=lambda k: (k % (groups // 4), k))
    order = []
    for i, k in enumerate(far):
        order.append(k)
        if i < len(near):
            order.append(near[i])
    return order


def fast_body(field):
    species, _, y_n, x_n = field.shape
    gz_n, gy_n = lax.axis_size("gz"), lax.axis_size("gy")
    total = gz_n * gy_n
    side = gy_n // CORES
    groups = gz_n * side
    grid_n = y_n * gy_n
    gz, gy = lax.axis_index("gz"), lax.axis_index("gy")
    me = gz * gy_n + gy
    core = gy % CORES
    group = (gz * side + gy // CORES).astype(jnp.int32)
    one = lambda v: jnp.reshape(v, (1,)).astype(jnp.int32)
    start_t = start_table(grid_n, RANK).T

    order = send_order(gz_n, side)
    pieces, recent = [], []
    gram = jnp.zeros((grid_n, grid_n), F32)
    source = field
    for s in range(species):
        if s:
            source = tie(source, recent[-len(order) // 2])
        sent = pack(source, one(group), s, groups)
        got = [sent[0]] + [None] * (groups - 1)
        for k in order:
            value = sent[k]
            if len(recent) >= DEPTH:
                value = tie(value, recent[-DEPTH])
            got[k] = permute(value, k * CORES, total)
            recent.append(got[k])
        pieces.append(got)
    for s in range(species):
        gram = gram_z_step(gram, pieces[s], one(group), side)
    gram = all_sum(gram, me, total, 4)
    basis_z, turned_z = leaf_basis(gram, start_t, one(gz), gz_n)

    side_pos = gy // CORES
    away = jnp.stack([1 - core, side_pos]).astype(jnp.int32)
    home = jnp.stack([core, side_pos]).astype(jnp.int32)
    leaving = [reduce_half(turned_z, pieces[s], away, side) for s in range(species)]
    others = [permute(value, 1, total) for value in leaving]
    mine = [reduce_half(turned_z, pieces[s], home, side) for s in range(species)]
    full, gram = gram_y_full(mine, others, one(core), side)
    gram = all_sum(gram, me, total, 4)
    basis_y, _ = leaf_basis(gram, start_t, one(gz), 1)
    core_tensor = project_core(basis_y, full)
    core_tensor = core_tensor.reshape(species, x_n // total, RANK * RANK)
    return core_tensor, basis_z.T, basis_y.T


def plain_basis(fibres, mode):
    highest = lax.Precision.HIGHEST
    others = tuple(d for d in range(4) if d != mode)
    gram = lax.dot_general(fibres, fibres, ((others, others), ((), ())), precision=highest)
    gram = lax.psum(gram, AXES)
    basis = start_table(gram.shape[0], RANK)
    for _ in range(ITERS):
        product = jnp.dot(gram, basis, precision=highest)
        inner = lax.dot_general(product, product, (((0,), (0,)), ((), ())), precision=highest)
        basis = lax.linalg.triangular_solve(
            jnp.linalg.cholesky(inner), product, left_side=False, lower=True, transpose_a=True)
    return basis


def plain_body(field):
    highest = lax.Precision.HIGHEST
    gz_n, gy_n = lax.axis_size("gz"), lax.axis_size("gy")
    fibres = lax.all_to_all(field, "gz", split_axis=2, concat_axis=1, tiled=True)
    basis_z = plain_basis(fibres, 1)
    reduced = jnp.einsum("szyx,zr->sryx", fibres, basis_z, precision=highest)
    mixed = lax.all_to_all(reduced, AXES, split_axis=3, concat_axis=2, tiled=True)
    shape = mixed.shape
    blocks = mixed.reshape(shape[0], shape[1], gz_n, gy_n, shape[2] // (gz_n * gy_n), shape[3])
    fibres = jnp.transpose(blocks, (0, 1, 3, 2, 4, 5)).reshape(shape)
    basis_y = plain_basis(fibres, 2)
    core_tensor = jnp.einsum("sryx,yq->sxrq", fibres, basis_y, precision=highest)
    return core_tensor.reshape(shape[0], shape[3], RANK * RANK), basis_z, basis_y


def body(field):
    gz_n, gy_n = lax.axis_size("gz"), lax.axis_size("gy")
    _, z_n, y_n, x_n = field.shape
    groups = gz_n * gy_n // CORES
    aligned = y_n % 128 == 0 and z_n % 64 == 0 and x_n % (8 * CORES * groups) == 0
    powers = gz_n % 4 == 0 and gz_n & (gz_n - 1) == 0 and gy_n >= 4 and gy_n & (gy_n - 1) == 0
    return fast_body(field) if aligned and powers else plain_body(field)


def solution(mesh):
    in_specs = (P(None, "gz", "gy", None),)
    out_specs = (P(None, AXES, None), P(), P())
    return jax.shard_map(body, mesh=mesh, in_specs=in_specs, out_specs=out_specs, check_vma=False)
```

```python
import functools
import math

import jax
import jax.numpy as jnp
from jax import lax
from jax.experimental import pallas as pl
from jax.experimental.pallas import tpu as pltpu
from jax.sharding import PartitionSpec as P

RANK = 64
ITERS = 4
CORES = 2
AXES = ("gz", "gy")
DEPTH = 6
PACK_AT = 9
REDUCE_X = 4
VMEM_LIMIT = 60 << 20
F32 = jnp.float32
BF16 = jnp.bfloat16


def start_table(order, width):
    row_index = jnp.arange(order).astype(jnp.float32)
    col_index = jnp.arange(width).astype(jnp.float32)
    return jnp.cos(math.pi * (row_index[:, None] + 0.5) * col_index[None, :] / order)


def tie(value, other):
    return lax.optimization_barrier((value, other))[0]


def split_bf16(value):
    high = value.astype(BF16)
    low = (value - high.astype(F32)).astype(BF16)
    return high, low


def dot_nn(left, right):
    return lax.dot_general(left, right, (((1,), (0,)), ((), ())), preferred_element_type=F32)


def dot_nt(left, right):
    return lax.dot_general(left, right, (((1,), (1,)), ((), ())), preferred_element_type=F32)


def dot_tn(left, right):
    return lax.dot_general(left, right, (((0,), (0,)), ((), ())), preferred_element_type=F32)


def pack_kernel(groups, width, me_ref, field_ref, *refs):
    out_refs, turned = refs[:-1], refs[-1]
    me = me_ref[0] % groups
    for z in range(field_ref.shape[1]):
        turned[...] = field_ref[0, z].T
        for k in range(groups):
            start = pl.multiple_of((me ^ k) * width, width)
            out_refs[k][:, z, :] = turned[pl.ds(start, width), :]


def pack(field, me_half, species, groups):
    _, z_n, y_n, x_n = field.shape
    width = x_n // (2 * groups)
    z_tile = 8
    return pl.pallas_call(
        functools.partial(pack_kernel, groups, width),
        grid_spec=pltpu.PrefetchScalarGridSpec(
            num_scalar_prefetch=1,
            grid=(z_n // z_tile,),
            in_specs=[pl.BlockSpec((1, z_tile, y_n, x_n // 2), lambda i, m: (species, i, 0, m[1]))],
            out_specs=[pl.BlockSpec((width, z_tile, y_n), lambda i, m: (0, i, 0))] * groups,
            scratch_shapes=[pltpu.VMEM((x_n // 2, y_n), F32)],
        ),
        out_shape=[jax.ShapeDtypeStruct((width, z_n, y_n), F32)] * groups,
        compiler_params=pltpu.CompilerParams(vmem_limit_bytes=VMEM_LIMIT),
        cost_estimate=pl.CostEstimate(
            flops=0, bytes_accessed=4 * z_n * y_n * x_n, transcendentals=0),
        name="pack",
    )(me_half, field)


def gram_z_kernel(groups, side, me_ref, prev_ref, *refs):
    pieces, out_ref, (high, low, sum_hh, sum_hl) = refs[:groups], refs[groups], refs[groups + 1:]
    step = pl.program_id(0)
    me_z = me_ref[0] // side
    x_tile, z_n, y_n = pieces[0].shape

    @pl.when(step == 0)
    def _():
        sum_hh[...] = jnp.zeros_like(sum_hh)
        sum_hl[...] = jnp.zeros_like(sum_hl)

    for k in range(groups):
        row = pl.multiple_of((me_z ^ (k // side)) * z_n, z_n)
        for x in range(x_tile):
            col = (x * side + k % side) * y_n
            high_part, low_part = split_bf16(pieces[k][x])
            high[pl.ds(row, z_n), col:col + y_n] = high_part
            low[pl.ds(row, z_n), col:col + y_n] = low_part
    sum_hh[...] += dot_nt(high[...], high[...])
    sum_hl[...] += dot_nt(high[...], low[...])

    @pl.when(step == pl.num_programs(0) - 1)
    def _():
        cross = sum_hl[...]
        out_ref[...] = prev_ref[...] + (sum_hh[...] + (cross + cross.T))


def gram_z_step(prev, pieces, me, side):
    groups = len(pieces)
    width, z_n, y_n = pieces[0].shape
    order = z_n * (groups // side)
    x_tile = 4
    depth = x_tile * side * y_n
    whole = pl.BlockSpec((order, order), lambda i, m: (0, 0))
    return pl.pallas_call(
        functools.partial(gram_z_kernel, groups, side),
        grid_spec=pltpu.PrefetchScalarGridSpec(
            num_scalar_prefetch=1,
            grid=(width // x_tile,),
            in_specs=[whole] + [pl.BlockSpec((x_tile, z_n, y_n), lambda i, m: (i, 0, 0))] * groups,
            out_specs=whole,
            scratch_shapes=[pltpu.VMEM((order, depth), BF16), pltpu.VMEM((order, depth), BF16),
                            pltpu.VMEM((order, order), F32), pltpu.VMEM((order, order), F32)],
        ),
        out_shape=jax.ShapeDtypeStruct((order, order), F32),
        compiler_params=pltpu.CompilerParams(vmem_limit_bytes=VMEM_LIMIT),
        cost_estimate=pl.CostEstimate(
            flops=4 * order * order * width * side * y_n,
            bytes_accessed=4 * groups * width * z_n * y_n, transcendentals=0),
        name="gram_z",
    )(me, prev, *pieces)


def split3(value):
    first = value.astype(BF16)
    rest = value - first.astype(F32)
    second = rest.astype(BF16)
    return first, second, (rest - second.astype(F32)).astype(BF16)


def dot_split(left, right, dot):
    rows = left[0].shape[0]
    first = dot(jnp.concatenate(left, axis=0), right[0])
    second = dot(jnp.concatenate(left[:2], axis=0), right[1])
    third = dot(left[0], right[2])
    small = first[2 * rows:] + second[rows:] + third
    return first[:rows] + (first[rows:2 * rows] + second[:rows] + small)


def inverse_factor(inner):
    rank = inner.shape[0]
    row_id = lax.broadcasted_iota(jnp.int32, (rank, 1), 0)
    rows = lax.broadcasted_iota(jnp.int32, (rank, 2 * rank), 0)
    lanes = lax.broadcasted_iota(jnp.int32, (rank, 2 * rank), 1)
    eye = jnp.where(lanes[:, :rank] == rows[:, :rank], 1.0, 0.0).astype(F32)
    work = jnp.concatenate([inner, eye], axis=1)
    for k in range(0, rank - 2, 2):
        col0 = jnp.broadcast_to(work[:, k:k + 1], work.shape)
        col1 = jnp.broadcast_to(work[:, k + 1:k + 2], work.shape)
        row0, row1 = work[k:k + 1, :], work[k + 1:k + 2, :]
        inv0 = 1.0 / col0[k:k + 1, :]
        share = col1[k:k + 1, :] * inv0
        inv1 = 1.0 / (col1[k + 1:k + 2, :] - col1[k:k + 1, :] * share)
        use1 = (row1 - share * row0) * inv1
        use0 = row0 * inv0 - share * use1
        below = row_id > k + 1
        work = work - (jnp.where(below, col0, 0.0) * use0 + jnp.where(below, col1, 0.0) * use1)
    take = lambda mask: jnp.sum(jnp.where(mask, work, 0.0), axis=1, keepdims=True)
    above = pltpu.roll(work, 1, 0)
    left = take(lanes == rows - 1)
    pivot_above = jnp.sum(jnp.where(lanes == rows - 1, above, 0.0), axis=1, keepdims=True)
    share = jnp.where(row_id % 2 == 1, left / jnp.where(row_id == 0, 1.0, pivot_above), 0.0)
    work = work - share * above
    return work[:, rank:] * (1.0 / jnp.sqrt(take(lanes == rows)))


def basis_kernel(gz_n, me_ref, gram_ref, start_ref, basis_ref, turned_ref, *parts):
    rank, order = start_ref.shape
    for ref, part in zip(parts, split3(gram_ref[...])):
        ref[...] = part

    def iterate(_, basis_t):
        product = dot_split(split3(basis_t), [ref[...] for ref in parts], dot_nn)
        pieces = split3(product)
        inner = dot_split(pieces, pieces, dot_nt)
        return dot_split(split3(inverse_factor(inner)), pieces, dot_nn)

    basis_t = lax.fori_loop(0, ITERS, iterate, start_ref[...])
    basis_ref[...] = basis_t
    if gz_n > 1:
        me_z = me_ref[0]
        size = order // gz_n
        while size < order:
            parts = [basis_t[:, i:i + size] for i in range(0, order, size)]
            swapped = jnp.concatenate([parts[i ^ 1] for i in range(len(parts))], axis=1)
            bit = (me_z // (size // (order // gz_n))) % 2
            basis_t = jnp.where(bit == 1, swapped, basis_t)
            size *= 2
    turned_ref[...] = basis_t


def leaf_basis(gram, start_t, me_z, gz_n):
    rank, order = start_t.shape
    vmem = pl.BlockSpec(memory_space=pltpu.VMEM)
    return pl.pallas_call(
        functools.partial(basis_kernel, gz_n),
        in_specs=[pl.BlockSpec(memory_space=pltpu.SMEM), vmem, vmem],
        out_specs=[vmem, vmem],
        out_shape=[jax.ShapeDtypeStruct((rank, order), F32)] * 2,
        scratch_shapes=[pltpu.VMEM((order, order), BF16)] * 3,
        compiler_params=pltpu.CompilerParams(vmem_limit_bytes=VMEM_LIMIT),
        name="leaf_basis",
    )(me_z, gram, start_t)


def reduce_kernel(species, groups, side, pos_ref, basis_ref, *refs):
    pieces, out_refs = refs[:species * groups], refs[species * groups:]
    rank = basis_ref.shape[0]
    me_x = pos_ref[1]
    x_tile, z_n, y_n = pieces[0].shape
    high, low = split_bf16(basis_ref[...])
    both = jnp.concatenate([high, low], axis=0)
    for s in range(species):
        for x in range(x_tile):
            cols = [jnp.concatenate([pieces[s * groups + k][x] for k in range(j, groups, side)], axis=0)
                    for j in range(side)]
            field_high, field_low = split_bf16(jnp.concatenate(cols, axis=1))
            first = dot_nn(both, field_high)
            total = first[:rank] + (first[rank:] + dot_nn(high, field_low))
            for j in range(side):
                start = pl.multiple_of((me_x ^ j) * y_n, y_n)
                out_refs[s][x, :, pl.ds(start, y_n)] = total[:, j * y_n:(j + 1) * y_n]


def reduce_half(basis_t, pieces, pos, side):
    species, groups = len(pieces), len(pieces[0])
    width, z_n, y_n = pieces[0][0].shape
    half = width // CORES
    x_tile = REDUCE_X
    rank, order = basis_t.shape
    tiles = half // x_tile
    return pl.pallas_call(
        functools.partial(reduce_kernel, species, groups, side),
        grid_spec=pltpu.PrefetchScalarGridSpec(
            num_scalar_prefetch=1,
            grid=(tiles,),
            in_specs=[pl.BlockSpec((rank, order), lambda i, p: (0, 0))]
            + [pl.BlockSpec((x_tile, z_n, y_n), lambda i, p: (p[0] * tiles + i, 0, 0))]
            * (species * groups),
            out_specs=[pl.BlockSpec((x_tile, rank, side * y_n), lambda i, p: (i, 0, 0))] * species,
        ),
        out_shape=[jax.ShapeDtypeStruct((half, rank, side * y_n), F32)] * species,
        compiler_params=pltpu.CompilerParams(vmem_limit_bytes=VMEM_LIMIT),
        cost_estimate=pl.CostEstimate(
            flops=6 * species * rank * order * half * side * y_n,
            bytes_accessed=4 * species * groups * half * z_n * y_n, transcendentals=0),
        name="reduce_z",
    )(pos, basis_t, *[piece for row in pieces for piece in row])


def gram_y_kernel(species, side, core_ref, *refs):
    mine, others = refs[:species], refs[species:2 * species]
    full_ref, gram_ref, sum_hh, sum_hl = refs[2 * species:]
    step = pl.program_id(0)
    core = core_ref[0]
    x_tile, rank, two = mine[0].shape
    y_n = two // side

    @pl.when(step == 0)
    def _():
        sum_hh[...] = jnp.zeros_like(sum_hh)
        sum_hl[...] = jnp.zeros_like(sum_hl)

    for s in range(species):
        for j in range(side):
            for ref, place in ((mine[s], core), (others[s], 1 - core)):
                start = pl.multiple_of((j * CORES + place) * y_n, y_n)
                full_ref[s, :, :, pl.ds(start, y_n)] = ref[:, :, j * y_n:(j + 1) * y_n]
    order = full_ref.shape[-1]
    high, low = split_bf16(full_ref[...].reshape(species * x_tile * rank, order))
    sum_hh[...] += dot_tn(high, high)
    sum_hl[...] += dot_tn(high, low)

    @pl.when(step == pl.num_programs(0) - 1)
    def _():
        cross = sum_hl[...]
        gram_ref[...] = sum_hh[...] + (cross + cross.T)


def gram_y_full(mine, others, core, side):
    species = len(mine)
    half, rank, two = mine[0].shape
    order = two * CORES
    x_tile = 4
    part = pl.BlockSpec((x_tile, rank, two), lambda i, c: (i, 0, 0))
    return pl.pallas_call(
        functools.partial(gram_y_kernel, species, side),
        grid_spec=pltpu.PrefetchScalarGridSpec(
            num_scalar_prefetch=1,
            grid=(half // x_tile,),
            in_specs=[part] * (2 * species),
            out_specs=[pl.BlockSpec((species, x_tile, rank, order), lambda i, c: (0, i, 0, 0)),
                       pl.BlockSpec((order, order), lambda i, c: (0, 0))],
            scratch_shapes=[pltpu.VMEM((order, order), F32), pltpu.VMEM((order, order), F32)],
        ),
        out_shape=[jax.ShapeDtypeStruct((species, half, rank, order), F32),
                   jax.ShapeDtypeStruct((order, order), F32)],
        compiler_params=pltpu.CompilerParams(vmem_limit_bytes=VMEM_LIMIT),
        name="gram_y",
    )(core, *mine, *others)


def core_kernel(basis_ref, full_ref, out_ref):
    species, x_tile, rank, order = full_ref.shape
    high, low = split_bf16(basis_ref[...])
    field_high, field_low = split_bf16(full_ref[...].reshape(species * x_tile * rank, order))
    first = dot_nt(field_high, jnp.concatenate([high, low], axis=0))
    second = dot_nt(field_low, high)
    total = first[:, :rank] + (first[:, rank:] + second)
    out_ref[...] = total.reshape(species, x_tile, rank, rank)


def project_core(basis_t, full):
    species, half, rank, order = full.shape
    x_tile = 4
    return pl.pallas_call(
        core_kernel,
        grid=(half // x_tile,),
        in_specs=[pl.BlockSpec((rank, order), lambda i: (0, 0)),
                  pl.BlockSpec((species, x_tile, rank, order), lambda i: (0, i, 0, 0))],
        out_specs=pl.BlockSpec((species, x_tile, rank, rank), lambda i: (0, i, 0, 0)),
        out_shape=jax.ShapeDtypeStruct((species, half, rank, rank), F32),
        compiler_params=pltpu.CompilerParams(vmem_limit_bytes=VMEM_LIMIT),
        name="core",
    )(basis_t, full)


def permute(value, mask, total):
    return lax.ppermute(value, AXES, [(i, i ^ mask) for i in range(total)])


def all_sum(value, me, total, quads):
    low = total // quads
    bits = [1 << b for b in range(low.bit_length() - 1)]
    current = value
    for bit in bits:
        half = current.shape[0] // 2
        upper = (me // bit) % 2 == 1
        first, second = current[:half], current[half:]
        current = jnp.where(upper, second, first) + permute(
            jnp.where(upper, first, second), bit, total)
    place = me // low
    parts = current.reshape(quads, -1, current.shape[1])
    pick = lambda k: lax.dynamic_index_in_dim(parts, place ^ k, 0, False)
    arrived = [permute(pick(k), low * k, total) for k in range(1, quads)]
    sums = pick(0)
    for part in arrived:
        sums = sums + part
    stack = jnp.stack([sums] + [permute(sums, low * k, total) for k in range(1, quads)])
    current = jnp.concatenate(
        [lax.dynamic_index_in_dim(stack, place ^ j, 0, False) for j in range(quads)])
    for bit in reversed(bits):
        other = permute(current, bit, total)
        upper = (me // bit) % 2 == 1
        current = jnp.concatenate(
            [jnp.where(upper, other, current), jnp.where(upper, current, other)])
    return current


def exchange(field, group, groups, total):
    half = groups // 2
    quarter = half // 2
    upper = group // half
    far_pos = jnp.stack([group, 1 - upper]).astype(jnp.int32)
    near_pos = jnp.stack([group, upper]).astype(jnp.int32)
    far_order = sorted(range(half), key=lambda k: (k % quarter, k))
    near_order = sorted(range(1, half), key=lambda k: ((k - 1) % quarter if k < quarter else k - quarter,
                                                       -k))
    recent, pieces = [], []
    source = field
    for s in range(field.shape[0]):
        if s:
            source = tie(source, recent[-PACK_AT])
        far = pack(source, far_pos, s, half)
        near = pack(tie(source, far[0]), near_pos, s, half)
        got = [near[0]] + [None] * (groups - 1)
        pieces.append(got)
        order = []
        for i, k in enumerate(far_order):
            order.append((half + k, far[k]))
            if i < len(near_order):
                order.append((near_order[i], near[near_order[i]]))
        for k, value in order:
            if len(recent) >= DEPTH:
                value = tie(value, recent[-DEPTH])
            got[k] = permute(value, k * CORES, total)
            recent.append(got[k])
    return pieces


def fast_body(field):
    species, _, y_n, x_n = field.shape
    gz_n, gy_n = lax.axis_size("gz"), lax.axis_size("gy")
    total = gz_n * gy_n
    side = gy_n // CORES
    groups = gz_n * side
    grid_n = y_n * gy_n
    gz, gy = lax.axis_index("gz"), lax.axis_index("gy")
    me = gz * gy_n + gy
    core = gy % CORES
    group = (gz * side + gy // CORES).astype(jnp.int32)
    one = lambda v: jnp.reshape(v, (1,)).astype(jnp.int32)
    start_t = start_table(grid_n, RANK).T

    pieces = exchange(field, group, groups, total)
    gram = jnp.zeros((grid_n, grid_n), F32)
    for s in range(species):
        gram = gram_z_step(gram, pieces[s], one(group), side)
    gram = all_sum(gram, me, total, 4)
    basis_z, turned_z = leaf_basis(gram, start_t, one(gz), gz_n)

    side_pos = gy // CORES
    away = jnp.stack([1 - core, side_pos]).astype(jnp.int32)
    home = jnp.stack([core, side_pos]).astype(jnp.int32)
    leaving = reduce_half(turned_z, pieces, away, side)
    others = [permute(value, 1, total) for value in leaving]
    mine = reduce_half(tie(turned_z, leaving[0]), pieces, home, side)
    full, gram = gram_y_full(mine, others, one(core), side)
    gram = all_sum(gram, me, total, 4)
    basis_y, _ = leaf_basis(gram, start_t, one(gz), 1)
    core_tensor = project_core(basis_y, full)
    core_tensor = core_tensor.reshape(species, x_n // total, RANK * RANK)
    return core_tensor, basis_z.T, basis_y.T


def plain_basis(fibres, mode):
    highest = lax.Precision.HIGHEST
    others = tuple(d for d in range(4) if d != mode)
    gram = lax.dot_general(fibres, fibres, ((others, others), ((), ())), precision=highest)
    gram = lax.psum(gram, AXES)
    basis = start_table(gram.shape[0], RANK)
    for _ in range(ITERS):
        product = jnp.dot(gram, basis, precision=highest)
        inner = lax.dot_general(product, product, (((0,), (0,)), ((), ())), precision=highest)
        basis = lax.linalg.triangular_solve(
            jnp.linalg.cholesky(inner), product, left_side=False, lower=True, transpose_a=True)
    return basis


def plain_body(field):
    highest = lax.Precision.HIGHEST
    gz_n, gy_n = lax.axis_size("gz"), lax.axis_size("gy")
    fibres = lax.all_to_all(field, "gz", split_axis=2, concat_axis=1, tiled=True)
    basis_z = plain_basis(fibres, 1)
    reduced = jnp.einsum("szyx,zr->sryx", fibres, basis_z, precision=highest)
    mixed = lax.all_to_all(reduced, AXES, split_axis=3, concat_axis=2, tiled=True)
    shape = mixed.shape
    blocks = mixed.reshape(shape[0], shape[1], gz_n, gy_n, shape[2] // (gz_n * gy_n), shape[3])
    fibres = jnp.transpose(blocks, (0, 1, 3, 2, 4, 5)).reshape(shape)
    basis_y = plain_basis(fibres, 2)
    core_tensor = jnp.einsum("sryx,yq->sxrq", fibres, basis_y, precision=highest)
    return core_tensor.reshape(shape[0], shape[3], RANK * RANK), basis_z, basis_y


def body(field):
    gz_n, gy_n = lax.axis_size("gz"), lax.axis_size("gy")
    _, z_n, y_n, x_n = field.shape
    groups = gz_n * gy_n // CORES
    aligned = y_n % 128 == 0 and z_n % 64 == 0 and x_n % (8 * CORES * groups) == 0
    powers = gz_n % 4 == 0 and gz_n & (gz_n - 1) == 0 and gy_n >= 4 and gy_n & (gy_n - 1) == 0
    return fast_body(field) if aligned and powers else plain_body(field)


def solution(mesh):
    in_specs = (P(None, "gz", "gy", None),)
    out_specs = (P(None, AXES, None), P(), P())
    return jax.shard_map(body, mesh=mesh, in_specs=in_specs, out_specs=out_specs, check_vma=False)
```

```python
import functools
import math

import jax
import jax.numpy as jnp
from jax import lax
from jax.experimental import pallas as pl
from jax.experimental.pallas import tpu as pltpu
from jax.sharding import PartitionSpec as P

RANK = 64
ITERS = 4
CORES = 2
AXES = ("gz", "gy")
DEPTH = 3
PACK_AT = 6
REDUCE_X = 4
GRAM_X = 4
GRAM_Y_X = 4
CORE_X = 8
VMEM_LIMIT = 60 << 20
F32 = jnp.float32
BF16 = jnp.bfloat16


def start_table(order, width):
    row_index = jnp.arange(order).astype(jnp.float32)
    col_index = jnp.arange(width).astype(jnp.float32)
    return jnp.cos(math.pi * (row_index[:, None] + 0.5) * col_index[None, :] / order)


def tie(value, other):
    return lax.optimization_barrier((value, other))[0]


def split_bf16(value):
    high = value.astype(BF16)
    low = (value - high.astype(F32)).astype(BF16)
    return high, low


def dot_nn(left, right):
    return lax.dot_general(left, right, (((1,), (0,)), ((), ())), preferred_element_type=F32)


def dot_nt(left, right):
    return lax.dot_general(left, right, (((1,), (1,)), ((), ())), preferred_element_type=F32)


def dot_tn(left, right):
    return lax.dot_general(left, right, (((0,), (0,)), ((), ())), preferred_element_type=F32)


def pack_kernel(count, width, pos_ref, field_ref, *refs):
    out_refs, turned = refs[:-1], refs[-1]
    me = pos_ref[0]
    for z in range(field_ref.shape[1]):
        turned[...] = field_ref[0, z].T
        for k in range(count):
            start = pl.multiple_of((me ^ k) * width, width)
            out_refs[k][:, z, :] = turned[pl.ds(start, width), :]


def pack(field, group, part, species, groups, parts):
    _, z_n, y_n, x_n = field.shape
    count, width = groups // parts, x_n // groups
    pos = jnp.stack([group % count, (group // count) ^ part]).astype(jnp.int32)
    z_tile = 8
    return pl.pallas_call(
        functools.partial(pack_kernel, count, width),
        grid_spec=pltpu.PrefetchScalarGridSpec(
            num_scalar_prefetch=1,
            grid=(z_n // z_tile,),
            in_specs=[pl.BlockSpec((1, z_tile, y_n, x_n // parts),
                                   lambda i, p: (species, i, 0, p[1]))],
            out_specs=[pl.BlockSpec((width, z_tile, y_n), lambda i, p: (0, i, 0))] * count,
            scratch_shapes=[pltpu.VMEM((x_n // parts, y_n), F32)],
        ),
        out_shape=[jax.ShapeDtypeStruct((width, z_n, y_n), F32)] * count,
        compiler_params=pltpu.CompilerParams(vmem_limit_bytes=VMEM_LIMIT),
        cost_estimate=pl.CostEstimate(
            flops=0, bytes_accessed=8 * z_n * y_n * x_n // parts, transcendentals=0),
        name="pack",
    )(pos, field)


def gram_z_kernel(groups, side, me_ref, prev_ref, *refs):
    pieces, out_ref, (high, low, sum_hh, sum_hl) = refs[:groups], refs[groups], refs[groups + 1:]
    step = pl.program_id(0)
    me_z = me_ref[0] // side
    x_tile, z_n, y_n = pieces[0].shape

    @pl.when(step == 0)
    def _():
        sum_hh[...] = jnp.zeros_like(sum_hh)
        sum_hl[...] = jnp.zeros_like(sum_hl)

    for k in range(groups):
        row = pl.multiple_of((me_z ^ (k // side)) * z_n, z_n)
        for x in range(x_tile):
            col = (x * side + k % side) * y_n
            high_part, low_part = split_bf16(pieces[k][x])
            high[pl.ds(row, z_n), col:col + y_n] = high_part
            low[pl.ds(row, z_n), col:col + y_n] = low_part
    sum_hh[...] += dot_nt(high[...], high[...])
    sum_hl[...] += dot_nt(high[...], low[...])

    @pl.when(step == pl.num_programs(0) - 1)
    def _():
        cross = sum_hl[...]
        out_ref[...] = prev_ref[...] + (sum_hh[...] + (cross + cross.T))


def gram_z_step(prev, pieces, me, side):
    groups = len(pieces)
    width, z_n, y_n = pieces[0].shape
    order = z_n * (groups // side)
    x_tile = GRAM_X
    depth = x_tile * side * y_n
    whole = pl.BlockSpec((order, order), lambda i, m: (0, 0))
    return pl.pallas_call(
        functools.partial(gram_z_kernel, groups, side),
        grid_spec=pltpu.PrefetchScalarGridSpec(
            num_scalar_prefetch=1,
            grid=(width // x_tile,),
            in_specs=[whole] + [pl.BlockSpec((x_tile, z_n, y_n), lambda i, m: (i, 0, 0))] * groups,
            out_specs=whole,
            scratch_shapes=[pltpu.VMEM((order, depth), BF16), pltpu.VMEM((order, depth), BF16),
                            pltpu.VMEM((order, order), F32), pltpu.VMEM((order, order), F32)],
        ),
        out_shape=jax.ShapeDtypeStruct((order, order), F32),
        compiler_params=pltpu.CompilerParams(vmem_limit_bytes=VMEM_LIMIT),
        cost_estimate=pl.CostEstimate(
            flops=4 * order * order * width * side * y_n,
            bytes_accessed=4 * groups * width * z_n * y_n, transcendentals=0),
        name="gram_z",
    )(me, prev, *pieces)


def split3(value):
    first = value.astype(BF16)
    rest = value - first.astype(F32)
    second = rest.astype(BF16)
    return first, second, (rest - second.astype(F32)).astype(BF16)


def dot_split(left, right, dot):
    rows = left[0].shape[0]
    first = dot(jnp.concatenate(left, axis=0), right[0])
    second = dot(jnp.concatenate(left[:2], axis=0), right[1])
    third = dot(left[0], right[2])
    small = first[2 * rows:] + second[rows:] + third
    return first[:rows] + (first[rows:2 * rows] + second[:rows] + small)


def inverse_factor(inner):
    rank = inner.shape[0]
    row_id = lax.broadcasted_iota(jnp.int32, (rank, 1), 0)
    rows = lax.broadcasted_iota(jnp.int32, (rank, 2 * rank), 0)
    lanes = lax.broadcasted_iota(jnp.int32, (rank, 2 * rank), 1)
    eye = jnp.where(lanes[:, :rank] == rows[:, :rank], 1.0, 0.0).astype(F32)
    work = jnp.concatenate([inner, eye], axis=1)
    for k in range(0, rank - 2, 2):
        col0 = jnp.broadcast_to(work[:, k:k + 1], work.shape)
        col1 = jnp.broadcast_to(work[:, k + 1:k + 2], work.shape)
        row0, row1 = work[k:k + 1, :], work[k + 1:k + 2, :]
        inv0 = 1.0 / col0[k:k + 1, :]
        share = col1[k:k + 1, :] * inv0
        inv1 = 1.0 / (col1[k + 1:k + 2, :] - col1[k:k + 1, :] * share)
        use1 = (row1 - share * row0) * inv1
        use0 = row0 * inv0 - share * use1
        below = row_id > k + 1
        work = work - (jnp.where(below, col0, 0.0) * use0 + jnp.where(below, col1, 0.0) * use1)
    take = lambda mask: jnp.sum(jnp.where(mask, work, 0.0), axis=1, keepdims=True)
    above = pltpu.roll(work, 1, 0)
    left = take(lanes == rows - 1)
    pivot_above = jnp.sum(jnp.where(lanes == rows - 1, above, 0.0), axis=1, keepdims=True)
    share = jnp.where(row_id % 2 == 1, left / jnp.where(row_id == 0, 1.0, pivot_above), 0.0)
    work = work - share * above
    return work[:, rank:] * (1.0 / jnp.sqrt(take(lanes == rows)))


def basis_kernel(gz_n, me_ref, gram_ref, start_ref, basis_ref, turned_ref, *parts):
    rank, order = start_ref.shape
    for ref, part in zip(parts, split3(gram_ref[...])):
        ref[...] = part

    def iterate(_, basis_t):
        product = dot_split(split3(basis_t), [ref[...] for ref in parts], dot_nn)
        pieces = split3(product)
        inner = dot_split(pieces, pieces, dot_nt)
        return dot_split(split3(inverse_factor(inner)), pieces, dot_nn)

    basis_t = lax.fori_loop(0, ITERS, iterate, start_ref[...])
    basis_ref[...] = basis_t
    if gz_n > 1:
        me_z = me_ref[0]
        size = order // gz_n
        while size < order:
            parts = [basis_t[:, i:i + size] for i in range(0, order, size)]
            swapped = jnp.concatenate([parts[i ^ 1] for i in range(len(parts))], axis=1)
            bit = (me_z // (size // (order // gz_n))) % 2
            basis_t = jnp.where(bit == 1, swapped, basis_t)
            size *= 2
    turned_ref[...] = basis_t


def leaf_basis(gram, start_t, me_z, gz_n):
    rank, order = start_t.shape
    vmem = pl.BlockSpec(memory_space=pltpu.VMEM)
    return pl.pallas_call(
        functools.partial(basis_kernel, gz_n),
        in_specs=[pl.BlockSpec(memory_space=pltpu.SMEM), vmem, vmem],
        out_specs=[vmem, vmem],
        out_shape=[jax.ShapeDtypeStruct((rank, order), F32)] * 2,
        scratch_shapes=[pltpu.VMEM((order, order), BF16)] * 3,
        compiler_params=pltpu.CompilerParams(vmem_limit_bytes=VMEM_LIMIT),
        name="leaf_basis",
    )(me_z, gram, start_t)


def reduce_kernel(species, groups, side, pos_ref, basis_ref, *refs):
    pieces, out_refs = refs[:species * groups], refs[species * groups:]
    rank = basis_ref.shape[0]
    me_x = pos_ref[1]
    x_tile, z_n, y_n = pieces[0].shape
    high, low = split_bf16(basis_ref[...])
    both = jnp.concatenate([high, low], axis=0)
    for s in range(species):
        for x in range(x_tile):
            cols = [jnp.concatenate([pieces[s * groups + k][x] for k in range(j, groups, side)], axis=0)
                    for j in range(side)]
            field_high, field_low = split_bf16(jnp.concatenate(cols, axis=1))
            first = dot_nn(both, field_high)
            total = first[:rank] + (first[rank:] + dot_nn(high, field_low))
            for j in range(side):
                start = pl.multiple_of((me_x ^ j) * y_n, y_n)
                out_refs[s][x, :, pl.ds(start, y_n)] = total[:, j * y_n:(j + 1) * y_n]


def reduce_half(basis_t, pieces, pos, side):
    species, groups = len(pieces), len(pieces[0])
    width, z_n, y_n = pieces[0][0].shape
    half = width // CORES
    x_tile = REDUCE_X
    rank, order = basis_t.shape
    tiles = half // x_tile
    return pl.pallas_call(
        functools.partial(reduce_kernel, species, groups, side),
        grid_spec=pltpu.PrefetchScalarGridSpec(
            num_scalar_prefetch=1,
            grid=(tiles,),
            in_specs=[pl.BlockSpec((rank, order), lambda i, p: (0, 0))]
            + [pl.BlockSpec((x_tile, z_n, y_n), lambda i, p: (p[0] * tiles + i, 0, 0))]
            * (species * groups),
            out_specs=[pl.BlockSpec((x_tile, rank, side * y_n), lambda i, p: (i, 0, 0))] * species,
        ),
        out_shape=[jax.ShapeDtypeStruct((half, rank, side * y_n), F32)] * species,
        compiler_params=pltpu.CompilerParams(vmem_limit_bytes=VMEM_LIMIT),
        cost_estimate=pl.CostEstimate(
            flops=6 * species * rank * order * half * side * y_n,
            bytes_accessed=4 * species * groups * half * z_n * y_n, transcendentals=0),
        name="reduce_z",
    )(pos, basis_t, *[piece for row in pieces for piece in row])


def gram_y_kernel(species, side, core_ref, *refs):
    mine, others = refs[:species], refs[species:2 * species]
    full_ref, gram_ref, sum_hh, sum_hl = refs[2 * species:]
    step = pl.program_id(0)
    core = core_ref[0]
    x_tile, rank, two = mine[0].shape
    y_n = two // side

    @pl.when(step == 0)
    def _():
        sum_hh[...] = jnp.zeros_like(sum_hh)
        sum_hl[...] = jnp.zeros_like(sum_hl)

    for s in range(species):
        for j in range(side):
            for ref, place in ((mine[s], core), (others[s], 1 - core)):
                start = pl.multiple_of((j * CORES + place) * y_n, y_n)
                full_ref[s, :, :, pl.ds(start, y_n)] = ref[:, :, j * y_n:(j + 1) * y_n]
    order = full_ref.shape[-1]
    high, low = split_bf16(full_ref[...].reshape(species * x_tile * rank, order))
    sum_hh[...] += dot_tn(high, high)
    sum_hl[...] += dot_tn(high, low)

    @pl.when(step == pl.num_programs(0) - 1)
    def _():
        cross = sum_hl[...]
        gram_ref[...] = sum_hh[...] + (cross + cross.T)


def gram_y_full(mine, others, core, side):
    species = len(mine)
    half, rank, two = mine[0].shape
    order = two * CORES
    x_tile = GRAM_Y_X
    part = pl.BlockSpec((x_tile, rank, two), lambda i, c: (i, 0, 0))
    return pl.pallas_call(
        functools.partial(gram_y_kernel, species, side),
        grid_spec=pltpu.PrefetchScalarGridSpec(
            num_scalar_prefetch=1,
            grid=(half // x_tile,),
            in_specs=[part] * (2 * species),
            out_specs=[pl.BlockSpec((species, x_tile, rank, order), lambda i, c: (0, i, 0, 0)),
                       pl.BlockSpec((order, order), lambda i, c: (0, 0))],
            scratch_shapes=[pltpu.VMEM((order, order), F32), pltpu.VMEM((order, order), F32)],
        ),
        out_shape=[jax.ShapeDtypeStruct((species, half, rank, order), F32),
                   jax.ShapeDtypeStruct((order, order), F32)],
        compiler_params=pltpu.CompilerParams(vmem_limit_bytes=VMEM_LIMIT),
        name="gram_y",
    )(core, *mine, *others)


def core_kernel(basis_ref, full_ref, out_ref):
    species, x_tile, rank, order = full_ref.shape
    high, low = split_bf16(basis_ref[...])
    field_high, field_low = split_bf16(full_ref[...].reshape(species * x_tile * rank, order))
    first = dot_nt(field_high, jnp.concatenate([high, low], axis=0))
    second = dot_nt(field_low, high)
    total = first[:, :rank] + (first[:, rank:] + second)
    out_ref[...] = total.reshape(species, x_tile, rank, rank)


def project_core(basis_t, full):
    species, half, rank, order = full.shape
    x_tile = CORE_X
    return pl.pallas_call(
        core_kernel,
        grid=(half // x_tile,),
        in_specs=[pl.BlockSpec((rank, order), lambda i: (0, 0)),
                  pl.BlockSpec((species, x_tile, rank, order), lambda i: (0, i, 0, 0))],
        out_specs=pl.BlockSpec((species, x_tile, rank, rank), lambda i: (0, i, 0, 0)),
        out_shape=jax.ShapeDtypeStruct((species, half, rank, rank), F32),
        compiler_params=pltpu.CompilerParams(vmem_limit_bytes=VMEM_LIMIT),
        name="core",
    )(basis_t, full)


def permute(value, mask, total):
    return lax.ppermute(value, AXES, [(i, i ^ mask) for i in range(total)])


def all_sum(value, me, total):
    stages = [(1, 2)]
    while stages[-1][0] * stages[-1][1] < total:
        step = stages[-1][0] * stages[-1][1]
        stages.append((step, min(4, total // step)))
    current = value
    for step, count in stages:
        place = (me // step) % count
        parts = current.reshape(count, -1, current.shape[1])
        pick = lambda k: lax.dynamic_index_in_dim(parts, place ^ k, 0, False)
        arrived = [permute(pick(k), step * k, total) for k in reversed(range(1, count))]
        current = pick(0)
        for part in reversed(arrived):
            current = current + part
    for step, count in reversed(stages):
        place = (me // step) % count
        got = [current] + [permute(current, step * k, total) for k in range(1, count)]
        if count == 2:
            swap = place == 1
            got = [jnp.where(swap, got[1], got[0]), jnp.where(swap, got[0], got[1])]
        else:
            stack = jnp.stack(got)
            got = [lax.dynamic_index_in_dim(stack, place ^ j, 0, False) for j in range(count)]
        current = jnp.concatenate(got)
    return current


def exchange(field, group, groups, total):
    half = groups // 2
    quarter = half // 2
    near_order = sorted(range(1, half), key=lambda k: ((k - 1) % quarter if k < quarter else k - quarter,
                                                       -k))
    done, pieces = [], []
    source = field
    for s in range(field.shape[0]):
        if s:
            source = tie(source, done[-PACK_AT][0])
        if s == 0:
            far_order = list(range(half))
            far = pack(source, group, 2, s, groups, 4)
            far = far + pack(tie(source, far[0]), group, 3, s, groups, 4)
        else:
            far_order = sorted(range(half), key=lambda k: (k % quarter, k))
            far = pack(source, group, 1, s, groups, 2)
        near = pack(tie(source, far[-1]), group, 0, s, groups, 2)
        got = [near[0]] + [None] * (groups - 1)
        pieces.append(got)
        for i, k in enumerate(far_order):
            pair = [(half + k, far[k])]
            if i < len(near_order):
                pair.append((near_order[i], near[near_order[i]]))
            values = [value for _, value in pair]
            if len(done) >= DEPTH:
                values = lax.optimization_barrier(values + done[-DEPTH])[:len(pair)]
            for (k, _), value in zip(pair, values):
                got[k] = permute(value, k * CORES, total)
            done.append([got[k] for k, _ in pair])
    return pieces


def fast_body(field):
    species, _, y_n, x_n = field.shape
    gz_n, gy_n = lax.axis_size("gz"), lax.axis_size("gy")
    total = gz_n * gy_n
    side = gy_n // CORES
    groups = gz_n * side
    grid_n = y_n * gy_n
    gz, gy = lax.axis_index("gz"), lax.axis_index("gy")
    me = gz * gy_n + gy
    core = gy % CORES
    group = (gz * side + gy // CORES).astype(jnp.int32)
    one = lambda v: jnp.reshape(v, (1,)).astype(jnp.int32)
    start_t = start_table(grid_n, RANK).T

    pieces = exchange(field, group, groups, total)
    gram = jnp.zeros((grid_n, grid_n), F32)
    for s in range(species):
        gram = gram_z_step(gram, pieces[s], one(group), side)
    gram = all_sum(gram, me, total)
    basis_z, turned_z = leaf_basis(gram, start_t, one(gz), gz_n)

    side_pos = gy // CORES
    away = jnp.stack([1 - core, side_pos]).astype(jnp.int32)
    home = jnp.stack([core, side_pos]).astype(jnp.int32)
    leaving = reduce_half(turned_z, pieces, away, side)
    others = [permute(value, 1, total) for value in leaving]
    mine = reduce_half(tie(turned_z, leaving[0]), pieces, home, side)
    full, gram = gram_y_full(mine, others, one(core), side)
    gram = all_sum(gram, me, total)
    basis_y, _ = leaf_basis(gram, start_t, one(gz), 1)
    core_tensor = project_core(basis_y, full)
    core_tensor = core_tensor.reshape(species, x_n // total, RANK * RANK)
    return core_tensor, basis_z.T, basis_y.T


def plain_basis(fibres, mode):
    highest = lax.Precision.HIGHEST
    others = tuple(d for d in range(4) if d != mode)
    gram = lax.dot_general(fibres, fibres, ((others, others), ((), ())), precision=highest)
    gram = lax.psum(gram, AXES)
    basis = start_table(gram.shape[0], RANK)
    for _ in range(ITERS):
        product = jnp.dot(gram, basis, precision=highest)
        inner = lax.dot_general(product, product, (((0,), (0,)), ((), ())), precision=highest)
        basis = lax.linalg.triangular_solve(
            jnp.linalg.cholesky(inner), product, left_side=False, lower=True, transpose_a=True)
    return basis


def plain_body(field):
    highest = lax.Precision.HIGHEST
    gz_n, gy_n = lax.axis_size("gz"), lax.axis_size("gy")
    fibres = lax.all_to_all(field, "gz", split_axis=2, concat_axis=1, tiled=True)
    basis_z = plain_basis(fibres, 1)
    reduced = jnp.einsum("szyx,zr->sryx", fibres, basis_z, precision=highest)
    mixed = lax.all_to_all(reduced, AXES, split_axis=3, concat_axis=2, tiled=True)
    shape = mixed.shape
    blocks = mixed.reshape(shape[0], shape[1], gz_n, gy_n, shape[2] // (gz_n * gy_n), shape[3])
    fibres = jnp.transpose(blocks, (0, 1, 3, 2, 4, 5)).reshape(shape)
    basis_y = plain_basis(fibres, 2)
    core_tensor = jnp.einsum("sryx,yq->sxrq", fibres, basis_y, precision=highest)
    return core_tensor.reshape(shape[0], shape[3], RANK * RANK), basis_z, basis_y


def body(field):
    gz_n, gy_n = lax.axis_size("gz"), lax.axis_size("gy")
    _, z_n, y_n, x_n = field.shape
    groups = gz_n * gy_n // CORES
    aligned = y_n % 128 == 0 and z_n % 64 == 0 and x_n % (8 * CORES * groups) == 0
    powers = gz_n % 4 == 0 and gz_n & (gz_n - 1) == 0 and gy_n >= 4 and gy_n & (gy_n - 1) == 0
    return fast_body(field) if aligned and powers else plain_body(field)


def solution(mesh):
    in_specs = (P(None, "gz", "gy", None),)
    out_specs = (P(None, AXES, None), P(), P())
    return jax.shard_map(body, mesh=mesh, in_specs=in_specs, out_specs=out_specs, check_vma=False)
```

```python
import functools
import math

import jax
import jax.numpy as jnp
from jax import lax
from jax.experimental import pallas as pl
from jax.experimental.pallas import tpu as pltpu
from jax.sharding import PartitionSpec as P

RANK = 64
ITERS = 4
CORES = 2
AXES = ("gz", "gy")
DEPTH = 3
PACK_AT = 6
REDUCE_X = 4
GRAM_X = 4
GRAM_Y_X = 4
CORE_X = 8
BLOCK = 8
VMEM_LIMIT = 60 << 20
F32 = jnp.float32
BF16 = jnp.bfloat16


def start_table(order, width):
    row_index = jnp.arange(order).astype(jnp.float32)
    col_index = jnp.arange(width).astype(jnp.float32)
    return jnp.cos(math.pi * (row_index[:, None] + 0.5) * col_index[None, :] / order)


def tie(value, other):
    return lax.optimization_barrier((value, other))[0]


def split_bf16(value):
    high = value.astype(BF16)
    low = (value - high.astype(F32)).astype(BF16)
    return high, low


def dot_nn(left, right):
    return lax.dot_general(left, right, (((1,), (0,)), ((), ())), preferred_element_type=F32)


def dot_nt(left, right):
    return lax.dot_general(left, right, (((1,), (1,)), ((), ())), preferred_element_type=F32)


def dot_tn(left, right):
    return lax.dot_general(left, right, (((0,), (0,)), ((), ())), preferred_element_type=F32)


def pack_kernel(count, width, pos_ref, field_ref, *refs):
    out_refs, turned = refs[:-1], refs[-1]
    me = pos_ref[0]
    for z in range(field_ref.shape[1]):
        turned[...] = field_ref[0, z].T
        for k in range(count):
            start = pl.multiple_of((me ^ k) * width, width)
            out_refs[k][:, z, :] = turned[pl.ds(start, width), :]


def pack(field, group, part, species, groups, parts):
    _, z_n, y_n, x_n = field.shape
    count, width = groups // parts, x_n // groups
    pos = jnp.stack([group % count, (group // count) ^ part]).astype(jnp.int32)
    z_tile = 8
    return pl.pallas_call(
        functools.partial(pack_kernel, count, width),
        grid_spec=pltpu.PrefetchScalarGridSpec(
            num_scalar_prefetch=1,
            grid=(z_n // z_tile,),
            in_specs=[pl.BlockSpec((1, z_tile, y_n, x_n // parts),
                                   lambda i, p: (species, i, 0, p[1]))],
            out_specs=[pl.BlockSpec((width, z_tile, y_n), lambda i, p: (0, i, 0))] * count,
            scratch_shapes=[pltpu.VMEM((x_n // parts, y_n), F32)],
        ),
        out_shape=[jax.ShapeDtypeStruct((width, z_n, y_n), F32)] * count,
        compiler_params=pltpu.CompilerParams(vmem_limit_bytes=VMEM_LIMIT),
        cost_estimate=pl.CostEstimate(
            flops=0, bytes_accessed=8 * z_n * y_n * x_n // parts, transcendentals=0),
        name="pack",
    )(pos, field)


def gram_z_kernel(groups, side, me_ref, prev_ref, *refs):
    pieces, out_ref, (high, low, sum_hh, sum_hl) = refs[:groups], refs[groups], refs[groups + 1:]
    step = pl.program_id(0)
    me_z = me_ref[0] // side
    x_tile, z_n, y_n = pieces[0].shape

    @pl.when(step == 0)
    def _():
        sum_hh[...] = jnp.zeros_like(sum_hh)
        sum_hl[...] = jnp.zeros_like(sum_hl)

    for k in range(groups):
        row = pl.multiple_of((me_z ^ (k // side)) * z_n, z_n)
        for x in range(x_tile):
            col = (x * side + k % side) * y_n
            high_part, low_part = split_bf16(pieces[k][x])
            high[pl.ds(row, z_n), col:col + y_n] = high_part
            low[pl.ds(row, z_n), col:col + y_n] = low_part
    sum_hh[...] += dot_nt(high[...], high[...])
    sum_hl[...] += dot_nt(high[...], low[...])

    @pl.when(step == pl.num_programs(0) - 1)
    def _():
        cross = sum_hl[...]
        out_ref[...] = prev_ref[...] + (sum_hh[...] + (cross + cross.T))


def gram_z_step(prev, pieces, me, side):
    groups = len(pieces)
    width, z_n, y_n = pieces[0].shape
    order = z_n * (groups // side)
    x_tile = GRAM_X
    depth = x_tile * side * y_n
    whole = pl.BlockSpec((order, order), lambda i, m: (0, 0))
    return pl.pallas_call(
        functools.partial(gram_z_kernel, groups, side),
        grid_spec=pltpu.PrefetchScalarGridSpec(
            num_scalar_prefetch=1,
            grid=(width // x_tile,),
            in_specs=[whole] + [pl.BlockSpec((x_tile, z_n, y_n), lambda i, m: (i, 0, 0))] * groups,
            out_specs=whole,
            scratch_shapes=[pltpu.VMEM((order, depth), BF16), pltpu.VMEM((order, depth), BF16),
                            pltpu.VMEM((order, order), F32), pltpu.VMEM((order, order), F32)],
        ),
        out_shape=jax.ShapeDtypeStruct((order, order), F32),
        compiler_params=pltpu.CompilerParams(vmem_limit_bytes=VMEM_LIMIT),
        cost_estimate=pl.CostEstimate(
            flops=4 * order * order * width * side * y_n,
            bytes_accessed=4 * groups * width * z_n * y_n, transcendentals=0),
        name="gram_z",
    )(me, prev, *pieces)


def split3(value):
    first = value.astype(BF16)
    rest = value - first.astype(F32)
    second = rest.astype(BF16)
    return first, second, (rest - second.astype(F32)).astype(BF16)


def dot_split(left, right, dot):
    rows = left[0].shape[0]
    first = dot(jnp.concatenate(left, axis=0), right[0])
    second = dot(jnp.concatenate(left[:2], axis=0), right[1])
    third = dot(left[0], right[2])
    small = first[2 * rows:] + second[rows:] + third
    return first[:rows] + (first[rows:2 * rows] + second[:rows] + small)


def inverse_factor(inner):
    rank = inner.shape[0]
    rows = lax.broadcasted_iota(jnp.int32, (rank, rank), 0)
    lanes = lax.broadcasted_iota(jnp.int32, (rank, rank), 1)
    eye = jnp.where(lanes == rows, 1.0, 0.0).astype(F32)
    work = jnp.concatenate([inner, eye], axis=1)
    finished = []
    for start in range(0, rank, BLOCK):
        cols = [jnp.broadcast_to(work[:, start + j:start + j + 1], work.shape) for j in range(BLOCK)]
        entry = {(i, j): cols[j][i:i + 1, :] for i in range(BLOCK) for j in range(i + 1)}
        row = [work[i:i + 1, :] for i in range(BLOCK)]
        scale, factor = [], {}
        for j in range(BLOCK):
            scale.append(1.0 / entry[j, j])
            finished.append((row[j] * (1.0 / jnp.sqrt(entry[j, j])))[:, rank:])
            for i in range(j + 1, BLOCK):
                factor[i, j] = entry[i, j] * scale[j]
            for i in range(j + 1, BLOCK):
                for t in range(j + 1, i + 1):
                    entry[i, t] = entry[i, t] - factor[i, j] * entry[t, j]
                row[i] = row[i] - factor[i, j] * row[j]
        if start + BLOCK == rank:
            break
        use = [row[j] * scale[j] for j in range(BLOCK)]
        for i in reversed(range(BLOCK)):
            for j in range(i):
                use[j] = use[j] - factor[i, j] * use[i]
        total = cols[0][BLOCK:] * use[0]
        for j in range(1, BLOCK):
            total = total + cols[j][BLOCK:] * use[j]
        work = work[BLOCK:] - total
    return jnp.concatenate(finished, axis=0)


def basis_kernel(gz_n, me_ref, gram_ref, start_ref, basis_ref, turned_ref, *parts):
    rank, order = start_ref.shape
    for ref, part in zip(parts, split3(gram_ref[...])):
        ref[...] = part

    def iterate(_, basis_t):
        product = dot_split(split3(basis_t), [ref[...] for ref in parts], dot_nn)
        pieces = split3(product)
        inner = dot_split(pieces, pieces, dot_nt)
        return dot_split(split3(inverse_factor(inner)), pieces, dot_nn)

    basis_t = lax.fori_loop(0, ITERS, iterate, start_ref[...])
    basis_ref[...] = basis_t
    if gz_n > 1:
        me_z = me_ref[0]
        size = order // gz_n
        while size < order:
            parts = [basis_t[:, i:i + size] for i in range(0, order, size)]
            swapped = jnp.concatenate([parts[i ^ 1] for i in range(len(parts))], axis=1)
            bit = (me_z // (size // (order // gz_n))) % 2
            basis_t = jnp.where(bit == 1, swapped, basis_t)
            size *= 2
    turned_ref[...] = basis_t


def leaf_basis(gram, start_t, me_z, gz_n):
    rank, order = start_t.shape
    vmem = pl.BlockSpec(memory_space=pltpu.VMEM)
    return pl.pallas_call(
        functools.partial(basis_kernel, gz_n),
        in_specs=[pl.BlockSpec(memory_space=pltpu.SMEM), vmem, vmem],
        out_specs=[vmem, vmem],
        out_shape=[jax.ShapeDtypeStruct((rank, order), F32)] * 2,
        scratch_shapes=[pltpu.VMEM((order, order), BF16)] * 3,
        compiler_params=pltpu.CompilerParams(vmem_limit_bytes=VMEM_LIMIT),
        name="leaf_basis",
    )(me_z, gram, start_t)


def reduce_kernel(species, groups, side, pos_ref, basis_ref, *refs):
    pieces, out_refs = refs[:species * groups], refs[species * groups:]
    rank = basis_ref.shape[0]
    me_x = pos_ref[1]
    x_tile, z_n, y_n = pieces[0].shape
    high, low = split_bf16(basis_ref[...])
    both = jnp.concatenate([high, low], axis=0)
    for s in range(species):
        for x in range(x_tile):
            cols = [jnp.concatenate([pieces[s * groups + k][x] for k in range(j, groups, side)], axis=0)
                    for j in range(side)]
            field_high, field_low = split_bf16(jnp.concatenate(cols, axis=1))
            first = dot_nn(both, field_high)
            total = first[:rank] + (first[rank:] + dot_nn(high, field_low))
            for j in range(side):
                start = pl.multiple_of((me_x ^ j) * y_n, y_n)
                out_refs[s][x, :, pl.ds(start, y_n)] = total[:, j * y_n:(j + 1) * y_n]


def reduce_half(basis_t, pieces, pos, side):
    species, groups = len(pieces), len(pieces[0])
    width, z_n, y_n = pieces[0][0].shape
    half = width // CORES
    x_tile = REDUCE_X
    rank, order = basis_t.shape
    tiles = half // x_tile
    return pl.pallas_call(
        functools.partial(reduce_kernel, species, groups, side),
        grid_spec=pltpu.PrefetchScalarGridSpec(
            num_scalar_prefetch=1,
            grid=(tiles,),
            in_specs=[pl.BlockSpec((rank, order), lambda i, p: (0, 0))]
            + [pl.BlockSpec((x_tile, z_n, y_n), lambda i, p: (p[0] * tiles + i, 0, 0))]
            * (species * groups),
            out_specs=[pl.BlockSpec((x_tile, rank, side * y_n), lambda i, p: (i, 0, 0))] * species,
        ),
        out_shape=[jax.ShapeDtypeStruct((half, rank, side * y_n), F32)] * species,
        compiler_params=pltpu.CompilerParams(vmem_limit_bytes=VMEM_LIMIT),
        cost_estimate=pl.CostEstimate(
            flops=6 * species * rank * order * half * side * y_n,
            bytes_accessed=4 * species * groups * half * z_n * y_n, transcendentals=0),
        name="reduce_z",
    )(pos, basis_t, *[piece for row in pieces for piece in row])


def gram_y_kernel(species, side, core_ref, *refs):
    mine, others = refs[:species], refs[species:2 * species]
    full_ref, gram_ref, sum_hh, sum_hl = refs[2 * species:]
    step = pl.program_id(0)
    core = core_ref[0]
    x_tile, rank, two = mine[0].shape
    y_n = two // side

    @pl.when(step == 0)
    def _():
        sum_hh[...] = jnp.zeros_like(sum_hh)
        sum_hl[...] = jnp.zeros_like(sum_hl)

    for s in range(species):
        for j in range(side):
            for ref, place in ((mine[s], core), (others[s], 1 - core)):
                start = pl.multiple_of((j * CORES + place) * y_n, y_n)
                full_ref[s, :, :, pl.ds(start, y_n)] = ref[:, :, j * y_n:(j + 1) * y_n]
    order = full_ref.shape[-1]
    high, low = split_bf16(full_ref[...].reshape(species * x_tile * rank, order))
    sum_hh[...] += dot_tn(high, high)
    sum_hl[...] += dot_tn(high, low)

    @pl.when(step == pl.num_programs(0) - 1)
    def _():
        cross = sum_hl[...]
        gram_ref[...] = sum_hh[...] + (cross + cross.T)


def gram_y_full(mine, others, core, side):
    species = len(mine)
    half, rank, two = mine[0].shape
    order = two * CORES
    x_tile = GRAM_Y_X
    part = pl.BlockSpec((x_tile, rank, two), lambda i, c: (i, 0, 0))
    return pl.pallas_call(
        functools.partial(gram_y_kernel, species, side),
        grid_spec=pltpu.PrefetchScalarGridSpec(
            num_scalar_prefetch=1,
            grid=(half // x_tile,),
            in_specs=[part] * (2 * species),
            out_specs=[pl.BlockSpec((species, x_tile, rank, order), lambda i, c: (0, i, 0, 0)),
                       pl.BlockSpec((order, order), lambda i, c: (0, 0))],
            scratch_shapes=[pltpu.VMEM((order, order), F32), pltpu.VMEM((order, order), F32)],
        ),
        out_shape=[jax.ShapeDtypeStruct((species, half, rank, order), F32),
                   jax.ShapeDtypeStruct((order, order), F32)],
        compiler_params=pltpu.CompilerParams(vmem_limit_bytes=VMEM_LIMIT),
        name="gram_y",
    )(core, *mine, *others)


def core_kernel(basis_ref, full_ref, out_ref):
    species, x_tile, rank, order = full_ref.shape
    high, low = split_bf16(basis_ref[...])
    field_high, field_low = split_bf16(full_ref[...].reshape(species * x_tile * rank, order))
    first = dot_nt(field_high, jnp.concatenate([high, low], axis=0))
    second = dot_nt(field_low, high)
    total = first[:, :rank] + (first[:, rank:] + second)
    out_ref[...] = total.reshape(species, x_tile, rank, rank)


def project_core(basis_t, full):
    species, half, rank, order = full.shape
    x_tile = CORE_X
    return pl.pallas_call(
        core_kernel,
        grid=(half // x_tile,),
        in_specs=[pl.BlockSpec((rank, order), lambda i: (0, 0)),
                  pl.BlockSpec((species, x_tile, rank, order), lambda i: (0, i, 0, 0))],
        out_specs=pl.BlockSpec((species, x_tile, rank, rank), lambda i: (0, i, 0, 0)),
        out_shape=jax.ShapeDtypeStruct((species, half, rank, rank), F32),
        compiler_params=pltpu.CompilerParams(vmem_limit_bytes=VMEM_LIMIT),
        name="core",
    )(basis_t, full)


def permute(value, mask, total):
    return lax.ppermute(value, AXES, [(i, i ^ mask) for i in range(total)])


def all_sum(value, me, total):
    stages = [(1, 2)]
    while stages[-1][0] * stages[-1][1] < total:
        step = stages[-1][0] * stages[-1][1]
        stages.append((step, min(4, total // step)))
    current = value
    for step, count in stages:
        place = (me // step) % count
        parts = current.reshape(count, -1, current.shape[1])
        pick = lambda k: lax.dynamic_index_in_dim(parts, place ^ k, 0, False)
        arrived = [permute(pick(k), step * k, total) for k in reversed(range(1, count))]
        current = pick(0)
        for part in reversed(arrived):
            current = current + part
    for step, count in reversed(stages):
        place = (me // step) % count
        got = [current] + [permute(current, step * k, total) for k in range(1, count)]
        if count == 2:
            swap = place == 1
            got = [jnp.where(swap, got[1], got[0]), jnp.where(swap, got[0], got[1])]
        else:
            stack = jnp.stack(got)
            got = [lax.dynamic_index_in_dim(stack, place ^ j, 0, False) for j in range(count)]
        current = jnp.concatenate(got)
    return current


def exchange(field, group, groups, total):
    half = groups // 2
    quarter = half // 2
    near_order = sorted(range(1, half), key=lambda k: ((k - 1) % quarter if k < quarter else k - quarter,
                                                       -k))
    done, pieces = [], []
    source = field
    for s in range(field.shape[0]):
        if s:
            source = tie(source, done[-PACK_AT][0])
        if s == 0:
            far_order = list(range(half))
            far = pack(source, group, 2, s, groups, 4)
            far = far + pack(tie(source, far[0]), group, 3, s, groups, 4)
        else:
            far_order = sorted(range(half), key=lambda k: (k % quarter, k))
            far = pack(source, group, 1, s, groups, 2)
        near = pack(tie(source, far[-1]), group, 0, s, groups, 2)
        got = [near[0]] + [None] * (groups - 1)
        pieces.append(got)
        for i, k in enumerate(far_order):
            pair = [(half + k, far[k])]
            if i < len(near_order):
                pair.append((near_order[i], near[near_order[i]]))
            values = [value for _, value in pair]
            if len(done) >= DEPTH:
                values = lax.optimization_barrier(values + done[-DEPTH])[:len(pair)]
            for (k, _), value in zip(pair, values):
                got[k] = permute(value, k * CORES, total)
            done.append([got[k] for k, _ in pair])
    return pieces


def fast_body(field):
    species, _, y_n, x_n = field.shape
    gz_n, gy_n = lax.axis_size("gz"), lax.axis_size("gy")
    total = gz_n * gy_n
    side = gy_n // CORES
    groups = gz_n * side
    grid_n = y_n * gy_n
    gz, gy = lax.axis_index("gz"), lax.axis_index("gy")
    me = gz * gy_n + gy
    core = gy % CORES
    group = (gz * side + gy // CORES).astype(jnp.int32)
    one = lambda v: jnp.reshape(v, (1,)).astype(jnp.int32)
    start_t = start_table(grid_n, RANK).T

    pieces = exchange(field, group, groups, total)
    gram = jnp.zeros((grid_n, grid_n), F32)
    for s in range(species):
        gram = gram_z_step(gram, pieces[s], one(group), side)
    gram = all_sum(gram, me, total)
    basis_z, turned_z = leaf_basis(gram, start_t, one(gz), gz_n)

    side_pos = gy // CORES
    away = jnp.stack([1 - core, side_pos]).astype(jnp.int32)
    home = jnp.stack([core, side_pos]).astype(jnp.int32)
    leaving = reduce_half(turned_z, pieces, away, side)
    others = [permute(value, 1, total) for value in leaving]
    mine = reduce_half(tie(turned_z, leaving[0]), pieces, home, side)
    full, gram = gram_y_full(mine, others, one(core), side)
    gram = all_sum(gram, me, total)
    basis_y, _ = leaf_basis(gram, start_t, one(gz), 1)
    core_tensor = project_core(basis_y, full)
    core_tensor = core_tensor.reshape(species, x_n // total, RANK * RANK)
    return core_tensor, basis_z.T, basis_y.T


def plain_basis(fibres, mode):
    highest = lax.Precision.HIGHEST
    others = tuple(d for d in range(4) if d != mode)
    gram = lax.dot_general(fibres, fibres, ((others, others), ((), ())), precision=highest)
    gram = lax.psum(gram, AXES)
    basis = start_table(gram.shape[0], RANK)
    for _ in range(ITERS):
        product = jnp.dot(gram, basis, precision=highest)
        inner = lax.dot_general(product, product, (((0,), (0,)), ((), ())), precision=highest)
        basis = lax.linalg.triangular_solve(
            jnp.linalg.cholesky(inner), product, left_side=False, lower=True, transpose_a=True)
    return basis


def plain_body(field):
    highest = lax.Precision.HIGHEST
    gz_n, gy_n = lax.axis_size("gz"), lax.axis_size("gy")
    fibres = lax.all_to_all(field, "gz", split_axis=2, concat_axis=1, tiled=True)
    basis_z = plain_basis(fibres, 1)
    reduced = jnp.einsum("szyx,zr->sryx", fibres, basis_z, precision=highest)
    mixed = lax.all_to_all(reduced, AXES, split_axis=3, concat_axis=2, tiled=True)
    shape = mixed.shape
    blocks = mixed.reshape(shape[0], shape[1], gz_n, gy_n, shape[2] // (gz_n * gy_n), shape[3])
    fibres = jnp.transpose(blocks, (0, 1, 3, 2, 4, 5)).reshape(shape)
    basis_y = plain_basis(fibres, 2)
    core_tensor = jnp.einsum("sryx,yq->sxrq", fibres, basis_y, precision=highest)
    return core_tensor.reshape(shape[0], shape[3], RANK * RANK), basis_z, basis_y


def body(field):
    gz_n, gy_n = lax.axis_size("gz"), lax.axis_size("gy")
    _, z_n, y_n, x_n = field.shape
    groups = gz_n * gy_n // CORES
    aligned = y_n % 128 == 0 and z_n % 64 == 0 and x_n % (8 * CORES * groups) == 0
    powers = gz_n % 4 == 0 and gz_n & (gz_n - 1) == 0 and gy_n >= 4 and gy_n & (gy_n - 1) == 0
    return fast_body(field) if aligned and powers else plain_body(field)


def solution(mesh):
    in_specs = (P(None, "gz", "gy", None),)
    out_specs = (P(None, AXES, None), P(), P())
    return jax.shard_map(body, mesh=mesh, in_specs=in_specs, out_specs=out_specs, check_vma=False)
```

```python
import functools
import math

import jax
import jax.numpy as jnp
from jax import lax
from jax.experimental import pallas as pl
from jax.experimental.pallas import tpu as pltpu
from jax.sharding import PartitionSpec as P

RANK = 64
ITERS = 4
CORES = 2
AXES = ("gz", "gy")
DEPTH = 3
PACK_AT = 6
REDUCE_X = 4
GRAM_X = 4
GRAM_Y_X = 4
CORE_X = 8
BLOCK = 8
VMEM_LIMIT = 60 << 20
F32 = jnp.float32
BF16 = jnp.bfloat16


def start_table(order, width):
    row_index = jnp.arange(order).astype(jnp.float32)
    col_index = jnp.arange(width).astype(jnp.float32)
    return jnp.cos(math.pi * (row_index[:, None] + 0.5) * col_index[None, :] / order)


def tie(value, other):
    return lax.optimization_barrier((value, other))[0]


def split_bf16(value):
    high = value.astype(BF16)
    low = (value - high.astype(F32)).astype(BF16)
    return high, low


def dot_nn(left, right):
    return lax.dot_general(left, right, (((1,), (0,)), ((), ())), preferred_element_type=F32)


def dot_nt(left, right):
    return lax.dot_general(left, right, (((1,), (1,)), ((), ())), preferred_element_type=F32)


def dot_tn(left, right):
    return lax.dot_general(left, right, (((0,), (0,)), ((), ())), preferred_element_type=F32)


def pack_kernel(count, width, pos_ref, field_ref, *refs):
    out_refs, turned = refs[:-1], refs[-1]
    me = pos_ref[0]
    for z in range(field_ref.shape[1]):
        turned[...] = field_ref[0, z].T
        for k in range(count):
            start = pl.multiple_of((me ^ k) * width, width)
            out_refs[k][:, z, :] = turned[pl.ds(start, width), :]


def pack(field, group, part, species, groups, parts):
    _, z_n, y_n, x_n = field.shape
    count, width = groups // parts, x_n // groups
    pos = jnp.stack([group % count, (group // count) ^ part]).astype(jnp.int32)
    z_tile = 8
    return pl.pallas_call(
        functools.partial(pack_kernel, count, width),
        grid_spec=pltpu.PrefetchScalarGridSpec(
            num_scalar_prefetch=1,
            grid=(z_n // z_tile,),
            in_specs=[pl.BlockSpec((1, z_tile, y_n, x_n // parts),
                                   lambda i, p: (species, i, 0, p[1]))],
            out_specs=[pl.BlockSpec((width, z_tile, y_n), lambda i, p: (0, i, 0))] * count,
            scratch_shapes=[pltpu.VMEM((x_n // parts, y_n), F32)],
        ),
        out_shape=[jax.ShapeDtypeStruct((width, z_n, y_n), F32)] * count,
        compiler_params=pltpu.CompilerParams(vmem_limit_bytes=VMEM_LIMIT),
        cost_estimate=pl.CostEstimate(
            flops=0, bytes_accessed=8 * z_n * y_n * x_n // parts, transcendentals=0),
        name="pack",
    )(pos, field)


def gram_z_kernel(groups, side, me_ref, prev_ref, *refs):
    pieces, out_refs, (high, low, sum_hh, sum_hl) = refs[:groups], refs[groups:-4], refs[-4:]
    step = pl.program_id(0)
    me_z = me_ref[0] // side
    x_tile, z_n, y_n = pieces[0].shape

    @pl.when(step == 0)
    def _():
        sum_hh[...] = jnp.zeros_like(sum_hh)
        sum_hl[...] = jnp.zeros_like(sum_hl)

    for k in range(groups):
        row = pl.multiple_of((me_z ^ (k // side)) * z_n, z_n)
        for x in range(x_tile):
            col = (x * side + k % side) * y_n
            high_part, low_part = split_bf16(pieces[k][x])
            high[pl.ds(row, z_n), col:col + y_n] = high_part
            low[pl.ds(row, z_n), col:col + y_n] = low_part
    sum_hh[...] += dot_nt(high[...], high[...])
    sum_hl[...] += dot_nt(high[...], low[...])

    @pl.when(step == pl.num_programs(0) - 1)
    def _():
        cross = sum_hl[...]
        sum_hh[...] = prev_ref[...] + (sum_hh[...] + (cross + cross.T))
        store_halves(out_refs, sum_hh, me_ref[1])


def store_halves(out_refs, full, core):
    rows = out_refs[0].shape[0]
    for i, ref in enumerate(out_refs):
        place = 0 if len(out_refs) == 1 else (core if i == 0 else 1 - core)
        ref[...] = full[pl.ds(pl.multiple_of(place * rows, rows), rows), :]


def gram_z_step(prev, pieces, me, side, halves):
    groups = len(pieces)
    width, z_n, y_n = pieces[0].shape
    order = z_n * (groups // side)
    x_tile = GRAM_X
    depth = x_tile * side * y_n
    whole = pl.BlockSpec((order, order), lambda i, m: (0, 0))
    return pl.pallas_call(
        functools.partial(gram_z_kernel, groups, side),
        grid_spec=pltpu.PrefetchScalarGridSpec(
            num_scalar_prefetch=1,
            grid=(width // x_tile,),
            in_specs=[whole] + [pl.BlockSpec((x_tile, z_n, y_n), lambda i, m: (i, 0, 0))] * groups,
            out_specs=[pl.BlockSpec((order // halves, order), lambda i, m: (0, 0))] * halves,
            scratch_shapes=[pltpu.VMEM((order, depth), BF16), pltpu.VMEM((order, depth), BF16),
                            pltpu.VMEM((order, order), F32), pltpu.VMEM((order, order), F32)],
        ),
        out_shape=[jax.ShapeDtypeStruct((order // halves, order), F32)] * halves,
        compiler_params=pltpu.CompilerParams(vmem_limit_bytes=VMEM_LIMIT),
        cost_estimate=pl.CostEstimate(
            flops=4 * order * order * width * side * y_n,
            bytes_accessed=4 * groups * width * z_n * y_n, transcendentals=0),
        name="gram_z",
    )(me, prev, *pieces)


def split3(value):
    first = value.astype(BF16)
    rest = value - first.astype(F32)
    second = rest.astype(BF16)
    return first, second, (rest - second.astype(F32)).astype(BF16)


def dot_split(left, right, dot):
    rows = left[0].shape[0]
    first = dot(jnp.concatenate(left, axis=0), right[0])
    second = dot(jnp.concatenate(left[:2], axis=0), right[1])
    third = dot(left[0], right[2])
    small = first[2 * rows:] + second[rows:] + third
    return first[:rows] + (first[rows:2 * rows] + second[:rows] + small)


def inverse_factor(inner):
    rank = inner.shape[0]
    rows = lax.broadcasted_iota(jnp.int32, (rank, rank), 0)
    lanes = lax.broadcasted_iota(jnp.int32, (rank, rank), 1)
    eye = jnp.where(lanes == rows, 1.0, 0.0).astype(F32)
    work = jnp.concatenate([inner, eye], axis=1)
    finished = []
    for start in range(0, rank, BLOCK):
        cols = [jnp.broadcast_to(work[:, start + j:start + j + 1], work.shape) for j in range(BLOCK)]
        entry = {(i, j): cols[j][i:i + 1, :] for i in range(BLOCK) for j in range(i + 1)}
        row = [work[i:i + 1, :] for i in range(BLOCK)]
        scale, factor = [], {}
        for j in range(BLOCK):
            scale.append(1.0 / entry[j, j])
            finished.append((row[j] * (1.0 / jnp.sqrt(entry[j, j])))[:, rank:])
            for i in range(j + 1, BLOCK):
                factor[i, j] = entry[i, j] * scale[j]
            for i in range(j + 1, BLOCK):
                for t in range(j + 1, i + 1):
                    entry[i, t] = entry[i, t] - factor[i, j] * entry[t, j]
                row[i] = row[i] - factor[i, j] * row[j]
        if start + BLOCK == rank:
            break
        use = [row[j] * scale[j] for j in range(BLOCK)]
        for i in reversed(range(BLOCK)):
            for j in range(i):
                use[j] = use[j] - factor[i, j] * use[i]
        total = cols[0][BLOCK:] * use[0]
        for j in range(1, BLOCK):
            total = total + cols[j][BLOCK:] * use[j]
        work = work[BLOCK:] - total
    return jnp.concatenate(finished, axis=0)


def basis_kernel(gz_n, me_ref, gram_ref, start_ref, basis_ref, turned_ref, *parts):
    rank, order = start_ref.shape
    for ref, part in zip(parts, split3(gram_ref[...])):
        ref[...] = part

    def iterate(_, basis_t):
        product = dot_split(split3(basis_t), [ref[...] for ref in parts], dot_nn)
        pieces = split3(product)
        inner = dot_split(pieces, pieces, dot_nt)
        return dot_split(split3(inverse_factor(inner)), pieces, dot_nn)

    basis_t = lax.fori_loop(0, ITERS, iterate, start_ref[...])
    basis_ref[...] = basis_t
    if gz_n > 1:
        me_z = me_ref[0]
        size = order // gz_n
        while size < order:
            parts = [basis_t[:, i:i + size] for i in range(0, order, size)]
            swapped = jnp.concatenate([parts[i ^ 1] for i in range(len(parts))], axis=1)
            bit = (me_z // (size // (order // gz_n))) % 2
            basis_t = jnp.where(bit == 1, swapped, basis_t)
            size *= 2
    turned_ref[...] = basis_t


def leaf_basis(gram, start_t, me_z, gz_n):
    rank, order = start_t.shape
    vmem = pl.BlockSpec(memory_space=pltpu.VMEM)
    return pl.pallas_call(
        functools.partial(basis_kernel, gz_n),
        in_specs=[pl.BlockSpec(memory_space=pltpu.SMEM), vmem, vmem],
        out_specs=[vmem, vmem],
        out_shape=[jax.ShapeDtypeStruct((rank, order), F32)] * 2,
        scratch_shapes=[pltpu.VMEM((order, order), BF16)] * 3,
        compiler_params=pltpu.CompilerParams(vmem_limit_bytes=VMEM_LIMIT),
        name="leaf_basis",
    )(me_z, gram, start_t)


def reduce_kernel(species, groups, side, pos_ref, basis_ref, *refs):
    pieces, out_refs = refs[:species * groups], refs[species * groups:]
    rank = basis_ref.shape[0]
    me_x = pos_ref[1]
    x_tile, z_n, y_n = pieces[0].shape
    high, low = split_bf16(basis_ref[...])
    both = jnp.concatenate([high, low], axis=0)
    for s in range(species):
        for x in range(x_tile):
            cols = [jnp.concatenate([pieces[s * groups + k][x] for k in range(j, groups, side)], axis=0)
                    for j in range(side)]
            field_high, field_low = split_bf16(jnp.concatenate(cols, axis=1))
            first = dot_nn(both, field_high)
            total = first[:rank] + (first[rank:] + dot_nn(high, field_low))
            for j in range(side):
                start = pl.multiple_of((me_x ^ j) * y_n, y_n)
                out_refs[s][x, :, pl.ds(start, y_n)] = total[:, j * y_n:(j + 1) * y_n]


def reduce_half(basis_t, pieces, pos, side):
    species, groups = len(pieces), len(pieces[0])
    width, z_n, y_n = pieces[0][0].shape
    half = width // CORES
    x_tile = REDUCE_X
    rank, order = basis_t.shape
    tiles = half // x_tile
    return pl.pallas_call(
        functools.partial(reduce_kernel, species, groups, side),
        grid_spec=pltpu.PrefetchScalarGridSpec(
            num_scalar_prefetch=1,
            grid=(tiles,),
            in_specs=[pl.BlockSpec((rank, order), lambda i, p: (0, 0))]
            + [pl.BlockSpec((x_tile, z_n, y_n), lambda i, p: (p[0] * tiles + i, 0, 0))]
            * (species * groups),
            out_specs=[pl.BlockSpec((x_tile, rank, side * y_n), lambda i, p: (i, 0, 0))] * species,
        ),
        out_shape=[jax.ShapeDtypeStruct((half, rank, side * y_n), F32)] * species,
        compiler_params=pltpu.CompilerParams(vmem_limit_bytes=VMEM_LIMIT),
        cost_estimate=pl.CostEstimate(
            flops=6 * species * rank * order * half * side * y_n,
            bytes_accessed=4 * species * groups * half * z_n * y_n, transcendentals=0),
        name="reduce_z",
    )(pos, basis_t, *[piece for row in pieces for piece in row])


def gram_y_kernel(species, side, core_ref, *refs):
    mine, others = refs[:species], refs[species:2 * species]
    full_ref, keep_ref, send_ref, sum_hh, sum_hl = refs[2 * species:]
    step = pl.program_id(0)
    core = core_ref[0]
    x_tile, rank, two = mine[0].shape
    y_n = two // side

    @pl.when(step == 0)
    def _():
        sum_hh[...] = jnp.zeros_like(sum_hh)
        sum_hl[...] = jnp.zeros_like(sum_hl)

    for s in range(species):
        for j in range(side):
            for ref, place in ((mine[s], core), (others[s], 1 - core)):
                start = pl.multiple_of((j * CORES + place) * y_n, y_n)
                full_ref[s, :, :, pl.ds(start, y_n)] = ref[:, :, j * y_n:(j + 1) * y_n]
    order = full_ref.shape[-1]
    high, low = split_bf16(full_ref[...].reshape(species * x_tile * rank, order))
    sum_hh[...] += dot_tn(high, high)
    sum_hl[...] += dot_tn(high, low)

    @pl.when(step == pl.num_programs(0) - 1)
    def _():
        cross = sum_hl[...]
        sum_hh[...] = sum_hh[...] + (cross + cross.T)
        store_halves((keep_ref, send_ref), sum_hh, core)


def gram_y_full(mine, others, core, side):
    species = len(mine)
    half, rank, two = mine[0].shape
    order = two * CORES
    x_tile = GRAM_Y_X
    part = pl.BlockSpec((x_tile, rank, two), lambda i, c: (i, 0, 0))
    return pl.pallas_call(
        functools.partial(gram_y_kernel, species, side),
        grid_spec=pltpu.PrefetchScalarGridSpec(
            num_scalar_prefetch=1,
            grid=(half // x_tile,),
            in_specs=[part] * (2 * species),
            out_specs=[pl.BlockSpec((species, x_tile, rank, order), lambda i, c: (0, i, 0, 0)),
                       *[pl.BlockSpec((order // CORES, order), lambda i, c: (0, 0))] * CORES],
            scratch_shapes=[pltpu.VMEM((order, order), F32), pltpu.VMEM((order, order), F32)],
        ),
        out_shape=[jax.ShapeDtypeStruct((species, half, rank, order), F32),
                   *[jax.ShapeDtypeStruct((order // CORES, order), F32)] * CORES],
        compiler_params=pltpu.CompilerParams(vmem_limit_bytes=VMEM_LIMIT),
        name="gram_y",
    )(core, *mine, *others)


def core_kernel(basis_ref, full_ref, out_ref):
    species, x_tile, rank, order = full_ref.shape
    high, low = split_bf16(basis_ref[...])
    field_high, field_low = split_bf16(full_ref[...].reshape(species * x_tile * rank, order))
    first = dot_nt(field_high, jnp.concatenate([high, low], axis=0))
    second = dot_nt(field_low, high)
    total = first[:, :rank] + (first[:, rank:] + second)
    out_ref[...] = total.reshape(species, x_tile, rank, rank)


def project_core(basis_t, full):
    species, half, rank, order = full.shape
    x_tile = CORE_X
    return pl.pallas_call(
        core_kernel,
        grid=(half // x_tile,),
        in_specs=[pl.BlockSpec((rank, order), lambda i: (0, 0)),
                  pl.BlockSpec((species, x_tile, rank, order), lambda i: (0, i, 0, 0))],
        out_specs=pl.BlockSpec((species, x_tile, rank, rank), lambda i: (0, i, 0, 0)),
        out_shape=jax.ShapeDtypeStruct((species, half, rank, rank), F32),
        compiler_params=pltpu.CompilerParams(vmem_limit_bytes=VMEM_LIMIT),
        name="core",
    )(basis_t, full)


def permute(value, mask, total):
    return lax.ppermute(value, AXES, [(i, i ^ mask) for i in range(total)])


def all_sum(keep, send, me, total):
    stages = []
    step = CORES
    while step < total:
        stages.append((step, min(4, total // step)))
        step *= stages[-1][1]
    current = keep + permute(send, 1, total)
    for step, count in stages:
        place = (me // step) % count
        parts = current.reshape(count, -1, current.shape[1])
        pick = lambda k: lax.dynamic_index_in_dim(parts, place ^ k, 0, False)
        arrived = [permute(pick(k), step * k, total) for k in reversed(range(1, count))]
        current = pick(0)
        for part in reversed(arrived):
            current = current + part
    for step, count in reversed(stages):
        place = (me // step) % count
        stack = jnp.stack([current] + [permute(current, step * k, total) for k in range(1, count)])
        current = jnp.concatenate(
            [lax.dynamic_index_in_dim(stack, place ^ j, 0, False) for j in range(count)])
    other = permute(current, 1, total)
    swap = me % CORES == 1
    return jnp.concatenate([jnp.where(swap, other, current), jnp.where(swap, current, other)])


def exchange(field, group, groups, total):
    half = groups // 2
    quarter = half // 2
    near_order = sorted(range(1, half), key=lambda k: ((k - 1) % quarter if k < quarter else k - quarter,
                                                       -k))
    done, pieces = [], []
    source = field
    for s in range(field.shape[0]):
        if s:
            source = tie(source, done[-PACK_AT][0])
        if s == 0:
            far_order = list(range(half))
            far = pack(source, group, 2, s, groups, 4)
            far = far + pack(tie(source, far[0]), group, 3, s, groups, 4)
        else:
            far_order = sorted(range(half), key=lambda k: (k % quarter, k))
            far = pack(source, group, 1, s, groups, 2)
        near = pack(tie(source, far[-1]), group, 0, s, groups, 2)
        got = [near[0]] + [None] * (groups - 1)
        pieces.append(got)
        for i, k in enumerate(far_order):
            pair = [(half + k, far[k])]
            if i < len(near_order):
                pair.append((near_order[i], near[near_order[i]]))
            values = [value for _, value in pair]
            if len(done) >= DEPTH:
                values = lax.optimization_barrier(values + done[-DEPTH])[:len(pair)]
            for (k, _), value in zip(pair, values):
                got[k] = permute(value, k * CORES, total)
            done.append([got[k] for k, _ in pair])
    return pieces


def fast_body(field):
    species, _, y_n, x_n = field.shape
    gz_n, gy_n = lax.axis_size("gz"), lax.axis_size("gy")
    total = gz_n * gy_n
    side = gy_n // CORES
    groups = gz_n * side
    grid_n = y_n * gy_n
    gz, gy = lax.axis_index("gz"), lax.axis_index("gy")
    me = gz * gy_n + gy
    core = gy % CORES
    group = (gz * side + gy // CORES).astype(jnp.int32)
    one = lambda v: jnp.reshape(v, (1,)).astype(jnp.int32)
    start_t = start_table(grid_n, RANK).T

    pieces = exchange(field, group, groups, total)
    gram = [jnp.zeros((grid_n, grid_n), F32)]
    place = jnp.stack([group, core]).astype(jnp.int32)
    for s in range(species):
        halves = CORES if s == species - 1 else 1
        gram = gram_z_step(gram[0], pieces[s], place, side, halves)
    gram = all_sum(*gram, me, total)
    basis_z, turned_z = leaf_basis(gram, start_t, one(gz), gz_n)

    side_pos = gy // CORES
    away = jnp.stack([1 - core, side_pos]).astype(jnp.int32)
    home = jnp.stack([core, side_pos]).astype(jnp.int32)
    leaving = reduce_half(turned_z, pieces, away, side)
    others = [permute(value, 1, total) for value in leaving]
    mine = reduce_half(tie(turned_z, leaving[0]), pieces, home, side)
    full, *gram = gram_y_full(mine, others, one(core), side)
    gram = all_sum(*gram, me, total)
    basis_y, _ = leaf_basis(gram, start_t, one(gz), 1)
    core_tensor = project_core(basis_y, full)
    core_tensor = core_tensor.reshape(species, x_n // total, RANK * RANK)
    return core_tensor, basis_z.T, basis_y.T


def plain_basis(fibres, mode):
    highest = lax.Precision.HIGHEST
    others = tuple(d for d in range(4) if d != mode)
    gram = lax.dot_general(fibres, fibres, ((others, others), ((), ())), precision=highest)
    gram = lax.psum(gram, AXES)
    basis = start_table(gram.shape[0], RANK)
    for _ in range(ITERS):
        product = jnp.dot(gram, basis, precision=highest)
        inner = lax.dot_general(product, product, (((0,), (0,)), ((), ())), precision=highest)
        basis = lax.linalg.triangular_solve(
            jnp.linalg.cholesky(inner), product, left_side=False, lower=True, transpose_a=True)
    return basis


def plain_body(field):
    highest = lax.Precision.HIGHEST
    gz_n, gy_n = lax.axis_size("gz"), lax.axis_size("gy")
    fibres = lax.all_to_all(field, "gz", split_axis=2, concat_axis=1, tiled=True)
    basis_z = plain_basis(fibres, 1)
    reduced = jnp.einsum("szyx,zr->sryx", fibres, basis_z, precision=highest)
    mixed = lax.all_to_all(reduced, AXES, split_axis=3, concat_axis=2, tiled=True)
    shape = mixed.shape
    blocks = mixed.reshape(shape[0], shape[1], gz_n, gy_n, shape[2] // (gz_n * gy_n), shape[3])
    fibres = jnp.transpose(blocks, (0, 1, 3, 2, 4, 5)).reshape(shape)
    basis_y = plain_basis(fibres, 2)
    core_tensor = jnp.einsum("sryx,yq->sxrq", fibres, basis_y, precision=highest)
    return core_tensor.reshape(shape[0], shape[3], RANK * RANK), basis_z, basis_y


def body(field):
    gz_n, gy_n = lax.axis_size("gz"), lax.axis_size("gy")
    _, z_n, y_n, x_n = field.shape
    groups = gz_n * gy_n // CORES
    aligned = y_n % 128 == 0 and z_n % 64 == 0 and x_n % (8 * CORES * groups) == 0
    powers = gz_n % 4 == 0 and gz_n & (gz_n - 1) == 0 and gy_n >= 4 and gy_n & (gy_n - 1) == 0
    return fast_body(field) if aligned and powers else plain_body(field)


def solution(mesh):
    in_specs = (P(None, "gz", "gy", None),)
    out_specs = (P(None, AXES, None), P(), P())
    return jax.shard_map(body, mesh=mesh, in_specs=in_specs, out_specs=out_specs, check_vma=False)
```
